256 devices in a mesh: date: 16 (over x, z_hi, core), col: 16 (over y, z_lo).
Axes of the slice: x: 4, y: 4, z: 8 (z_hi: 2, z_lo: 4; z = z_hi * 4 + z_lo), core: 2. Of those that a mesh axis runs over, the one named last changes fastest.
Arguments:
- slc: float32 [80, 2, 40, 40960], P('date', None, None, 'col'), as said below
- pairs: int32 [160, 2], replicated, may hold values from 0 to 79, as said below
Outputs:
- interferogram: float32 [160, 2, 8, 2048], P('date', None, None, 'col')
- coherence: float32 [160, 8, 2048], P('date', None, 'col')
The draws below stay inside these ranges and needn't reach their ends.
Inputs may be any that keep to these rules, and one draw needn't show every extreme that they name: `pairs`: rows 2i and 2i+1 have reference date i; each secondary date differs from its reference by 1 to 5 dates, and some pair differs by exactly 5. `slc`: every pixel's magnitude is at least 0.1.
All inputs are finite; a program needn't handle non-finite values.
Results may differ from the reference program's by a relative error of at most 0.00002.
Values sent between devices are 32-bit elements; how exact they have to be, the bound alone decides.
A program may use at most 128 MiB of HBM per device.

```python
import math
import jax
import jax.numpy as jnp
from jax import lax

ROWS = 40
GAP = 5
WIN = 11
LOOK_R = 5
LOOK_C = 20
DATES = 80
COLS = 40960


def draw_slc(key, part):
    key = jax.random.fold_in(key, 11)
    key_amp = jax.random.fold_in(key, 0)
    key_psi = jax.random.fold_in(key, 1)
    key_level = jax.random.fold_in(key, 2)
    key_noise = jax.random.fold_in(key, 3)
    key_gain = jax.random.fold_in(key, 5)
    key_pixel = jax.random.fold_in(key, 6)
    amplitude = jnp.exp(jax.random.uniform(key_amp, (ROWS, COLS), jnp.float32, math.log(0.3), math.log(3.0)))
    date_gain = jnp.exp(jax.random.uniform(key_gain, (DATES, 1, 1), jnp.float32, -math.log(2.0), math.log(2.0)))
    pixel_gain = jnp.exp(jax.random.uniform(key_pixel, (DATES, ROWS, COLS), jnp.float32, -math.log(1.5), math.log(1.5)))
    magnitude = amplitude[None] * date_gain * pixel_gain
    scene = jax.random.uniform(key_psi, (ROWS, COLS), jnp.float32, -math.pi, math.pi)
    level = jax.random.uniform(key_level, (ROWS, COLS), jnp.float32, 0.1, 1.0)
    noise = jax.random.uniform(key_noise, (DATES, ROWS, COLS), jnp.float32, -1.0, 1.0)
    phase = scene[None] + math.pi * level[None] * noise
    return jnp.stack([magnitude * jnp.cos(phase), magnitude * jnp.sin(phase)], axis=1).astype(jnp.float32)


def draw_pairs(key, part):
    key = jax.random.fold_in(key, 23)
    key_fwd, key_back = jax.random.split(key, 2)
    forward = jax.random.randint(key_fwd, (DATES,), 1, GAP + 1).astype(jnp.int32)
    forward = forward.at[0].set(GAP)
    backward = jax.random.randint(key_back, (DATES,), 1, GAP + 1).astype(jnp.int32)
    index = jnp.arange(DATES, dtype=jnp.int32)
    later = jnp.where(index + forward < DATES, index + forward, index - forward)
    earlier = jnp.where(index - backward >= 0, index - backward, index + backward)
    second = jnp.stack([later, earlier], axis=1).reshape(-1)
    first = jnp.repeat(index, 2)
    return jnp.stack([first, second], axis=1).astype(jnp.int32)


def setup_inputs(seed: int = 0) -> dict:
    keys = jax.random.split(jax.random.key(seed), 3)
    return {
        "slc": draw_slc(jax.random.fold_in(keys[2], 71), 0),
        "pairs": draw_pairs(jax.random.fold_in(keys[2], 71), 0),
    }


def box_sum(field):
    half = WIN // 2
    rows = field.shape[-2]
    width = field.shape[-1] - 2 * half
    padded = jnp.pad(field, [(0, 0)] * (field.ndim - 2) + [(half, half), (0, 0)])
    total = padded[..., 0:rows, :]
    for shift_k in range(1, WIN):
        total = total + padded[..., shift_k:shift_k + rows, :]
    result = total[..., 0:width]
    for shift_k in range(1, WIN):
        result = result + total[..., shift_k:shift_k + width]
    return result

def look_mean(field):
    rows, width = field.shape
    blocks = field.reshape(rows // LOOK_R, LOOK_R, width // LOOK_C, LOOK_C)
    return lax.optimization_barrier(jnp.sum(blocks, axis=(1, 3))) / float(LOOK_R * LOOK_C)

def pair_result(first, second, power_first, power_second):
    half = WIN // 2
    width = first.shape[-1] - 2 * half
    real_part = first[0] * second[0] + first[1] * second[1]
    imag_part = first[1] * second[0] - first[0] * second[1]
    sum_re = box_sum(real_part)
    sum_im = box_sum(imag_part)
    pixel_coh = jnp.sqrt(sum_re * sum_re + sum_im * sum_im) / jnp.sqrt(power_first * power_second)
    inner_re = real_part[:, half:half + width]
    inner_im = imag_part[:, half:half + width]
    ifg = jnp.stack([look_mean(inner_re), look_mean(inner_im)], axis=0)
    return (ifg, look_mean(pixel_coh))

def reference(slc, pairs):
    half = WIN // 2

    def one_pair(pair_row):
        first = jnp.pad(slc[pair_row[0]], ((0, 0), (0, 0), (half, half)))
        second = jnp.pad(slc[pair_row[1]], ((0, 0), (0, 0), (half, half)))
        power_first = box_sum(first[0] * first[0] + first[1] * first[1])
        power_second = box_sum(second[0] * second[0] + second[1] * second[1])
        return pair_result(first, second, power_first, power_second)
    interferogram, coherence = lax.map(one_pair, pairs)
    return (interferogram, coherence)
```

```python
import functools

import jax
import jax.numpy as jnp
from jax import lax
from jax.experimental import pallas as pl
from jax.experimental.pallas import tpu as pltpu
from jax.sharding import PartitionSpec as P

GAP = 5
HALF = 5
ROWS = 40
WIDTH = 2560
BLOCK = 256
BLOCKS = WIDTH // BLOCK
LOOK_C = 20
MESH = pl.DeviceIdType.MESH
F32 = jnp.float32
BF16 = jnp.bfloat16


def plan_kernel(pairs_ref, tab_ref):
    rows = pairs_ref.shape[0]
    lane = lax.broadcasted_iota(jnp.int32, (rows, 128), 1)
    row = lax.broadcasted_iota(jnp.int32, (rows, 128), 0)
    second = jnp.broadcast_to(pairs_ref[:, 1:2], (rows, 128))
    lane8 = lax.broadcasted_iota(jnp.int32, (8, 128), 1)
    row8 = lax.broadcasted_iota(jnp.int32, (8, 128), 0)
    sec, dist = [], []
    for q in range(2):
        s = jnp.sum(jnp.where(row == 2 * lane + q, second, 0), axis=0, keepdims=True)
        s = jnp.broadcast_to(s, (8, 128))
        sec.append(s)
        dist.append(jnp.where(lane8 < rows // 2, s - lane8, 0))
    up = jnp.zeros((8, 128), jnp.int32)
    for k in range(1, GAP + 1):
        fwd = jnp.where((dist[0] == k) | (dist[1] == k), 1, 0)
        back = jnp.where((dist[0] == -k) | (dist[1] == -k), 1, 0)
        up = up | ((fwd | pltpu.roll(back, 128 - k, 1)) << (k - 1))
    masks = [pltpu.roll(up, GAP - i, 1) >> (GAP - 1 - i) for i in range(GAP)]
    found = jnp.zeros((8, 128), jnp.int32)
    s0 = jnp.zeros((8, 128), jnp.int32)
    s1 = jnp.ones((8, 128), jnp.int32)
    need = jnp.zeros((8, 128), jnp.int32)
    for lo in range(GAP - 2, -1, -1):
        for hi in range(GAP - 1, lo, -1):
            rest = jnp.zeros((8, 128), jnp.int32)
            for i in range(GAP):
                if i not in (lo, hi):
                    rest = rest | masks[i]
            count = jnp.zeros((8, 128), jnp.int32)
            for j in range(GAP):
                count = count + ((rest >> j) & 1)
            take = (count <= 2) & (found == 0)
            s0 = jnp.where(take, lo, s0)
            s1 = jnp.where(take, hi, s1)
            need = jnp.where(take, rest, need)
            found = jnp.where(take, 1, found)
    t0 = jnp.zeros((8, 128), jnp.int32)
    t1 = jnp.zeros((8, 128), jnp.int32)
    for j in range(GAP):
        t1 = jnp.where(((need >> j) & 1) == 1, j, t1)
        t0 = jnp.where(((need >> (GAP - 1 - j)) & 1) == 1, GAP - 1 - j, t0)
    chip = (lane8 % (2 * GAP) == 0) & (lane8 > 0) & (lane8 < rows // 2)
    missing = jnp.where(chip & (found == 0), 1.0, 0.0)
    wide = jnp.broadcast_to(jnp.max(missing, axis=1, keepdims=True), (8, 128)) > 0.5
    picks = [
        jnp.where(wide, 2, s0),
        jnp.where(wide, 3, s1),
        jnp.where(wide, 4, 0),
        jnp.where(wide, 0, t0),
        jnp.where(wide, 1, t1),
        jnp.zeros((8, 128), jnp.int32),
        sec[0],
        sec[1],
    ]
    table = jnp.zeros((8, 128), jnp.int32)
    for r, value in enumerate(picks):
        table = jnp.where(row8 == r, value, table)
    tab_ref[...] = jnp.where((lane8 == 127) & (row8 == 0), jnp.where(wide, 1, 0), table)


def split(x):
    hi = x.astype(BF16)
    return hi, (x - hi.astype(F32)).astype(BF16)


def row_window(x):
    x = jnp.concatenate([x, jnp.zeros((8, x.shape[1]), F32)], axis=0)
    n = x.shape[0]
    two = x + pltpu.roll(x, n - 1, 0)
    four = two + pltpu.roll(two, n - 2, 0)
    eight = four + pltpu.roll(four, n - 4, 0)
    total = eight + pltpu.roll(two, n - 8, 0) + pltpu.roll(x, n - 10, 0)
    return pltpu.roll(total, HALF, 0)[:ROWS]


def dot(a, b):
    return jnp.dot(a, b, preferred_element_type=F32)


def main_kernel(
    cross, tab, slc, out_ifg, out_coh,
    own, dates, sent, stage, hi_buf, lo_buf, inv, acc_ifg, acc_coh, look_i, look_c, band,
    edge, halo, other, tiles, tiles_nb, res, res_far, res_in, plan,
    load_sem, sib_send, sib_recv, nb_send, nb_recv, edge_send, edge_recv, halo_send, halo_recv, res_send, res_recv,
):
    held = stage.shape[0]
    starts = GAP + cross
    power_rows = held * ROWS
    d, c = lax.axis_index("date"), lax.axis_index("col")
    n_d, n_c = lax.axis_size("date"), lax.axis_size("col")
    odd = lax.rem(d, 2)
    sib = d + 1 - 2 * odd
    nb = d - 1 + 2 * odd
    has_nb = (nb >= 0) & (nb < n_d)
    has_left, has_right = c > 0, c < n_c - 1

    load = pltpu.make_async_copy(slc, own, load_sem)
    load.start()

    barrier = pltpu.get_barrier_semaphore()
    pl.semaphore_signal(barrier, inc=1, device_id=(sib, c), device_id_type=MESH)

    @pl.when(has_nb)
    def _():
        pl.semaphore_signal(barrier, inc=1, device_id=(nb, c), device_id_type=MESH)

    @pl.when(has_left)
    def _():
        pl.semaphore_signal(barrier, inc=1, device_id=(d, c - 1), device_id_type=MESH)

    @pl.when(has_right)
    def _():
        pl.semaphore_signal(barrier, inc=1, device_id=(d, c + 1), device_id_type=MESH)

    lane_of = 5 * (d + odd)
    sel_out = [tab[3 * (1 - odd) + s, lane_of] for s in range(cross)]
    sel_in = [tab[3 * odd + s, lane_of] for s in range(cross)]
    for r in range(GAP):
        for q in range(2):
            b = tab[6 + q, GAP * d + r]
            mine, sibling, far = b - GAP * d, b - GAP * sib, b - GAP * nb
            in_own = (mine >= 0) & (mine < GAP)
            in_sib = (sibling >= 0) & (sibling < GAP)
            place, here, back = jnp.int32(0), jnp.int32(0), jnp.int32(0)
            for s in range(cross):
                match = has_nb & (sel_in[s] == far)
                place = jnp.where(match, 2 * GAP + s, place)
                here = jnp.where(match, 1, here)
                back = jnp.where(sel_out[s] == r, 2 * s + q, back)
            place = jnp.where(in_own, mine, jnp.where(in_sib, GAP + sibling, place))
            here = jnp.where(in_own | in_sib, 1, here)
            plan[0, 2 * r + q] = place
            plan[1, 2 * r + q] = here
            plan[2, 2 * r + q] = back
    for s in range(cross):
        for q in range(2):
            far_date = jnp.clip(GAP * nb + sel_in[s], 0, GAP * n_d - 1)
            mine = tab[6 + q, far_date] - GAP * d
            plan[0, 2 * (GAP + s) + q] = jnp.where((mine >= 0) & (mine < GAP), mine, 0)

    k = lax.broadcasted_iota(jnp.int32, (BLOCK, BLOCK), 0)
    n = lax.broadcasted_iota(jnp.int32, (BLOCK, BLOCK), 1)
    near = lambda x: jnp.abs(x) <= HALF
    left_half = n < BLOCK // 2
    wrapped = jnp.where(
        left_half,
        jnp.where((k >= 246) & (k < 251) & near(k - 246 - (n - 128)), 1.0, 0.0),
        jnp.where(((k < 246) & near(k - n + 128)) | ((k >= 251) & near(k - 256 - n + 128)), 1.0, 0.0),
    )
    band[0] = jnp.where(near(k - n + 128), 1.0, 0.0).astype(BF16)
    band[1] = jnp.where(near(k - n - 128), 1.0, 0.0).astype(BF16)
    band[2] = wrapped.astype(BF16)
    band[3] = jnp.where(left_half & near(k - n - 128), 1.0, 0.0).astype(BF16)

    def fill_look(j, carry):
        column = lax.broadcasted_iota(jnp.int32, (BLOCK, 128), 0) + j * BLOCK
        first = lax.broadcasted_iota(jnp.int32, (BLOCK, 128), 1) * LOOK_C
        at = column - first
        look_i[j] = jnp.where((at >= 0) & (at < LOOK_C), 1.0, 0.0).astype(BF16)
        at = column - BLOCK // 2
        at = jnp.where(at >= WIDTH, at - WIDTH, at) - first
        look_c[j] = jnp.where((at >= 0) & (at < LOOK_C), 1.0, 0.0).astype(BF16)
        return carry

    lax.fori_loop(0, BLOCKS + 1, fill_look, 0)
    acc_ifg[...] = jnp.zeros_like(acc_ifg)
    acc_coh[...] = jnp.zeros_like(acc_coh)

    @pl.when(jnp.logical_not(has_nb))
    def _():
        dates[GAP : GAP + cross] = jnp.zeros((cross, 2, ROWS, WIDTH), F32)
        other[1] = jnp.zeros((ROWS, 128), F32)
        res_in[...] = jnp.zeros_like(res_in)

    if held > 2 * GAP + cross:
        stage[held - 1] = jnp.zeros((2, ROWS, BLOCK), F32)
        tiles[held - 1] = jnp.zeros((2, ROWS, 128), F32)

    pl.semaphore_wait(
        barrier, 1 + has_nb.astype(jnp.int32) + has_left.astype(jnp.int32) + has_right.astype(jnp.int32)
    )
    load.wait()

    def at_block(j):
        return pl.ds(pl.multiple_of(j * BLOCK, BLOCK), BLOCK)

    def to_sib(j):
        return pltpu.make_async_remote_copy(
            own.at[:, :, :, at_block(j)], dates.at[0:GAP, :, :, at_block(j)],
            sib_send.at[j], sib_recv.at[j], device_id=(sib, c), device_id_type=MESH,
        )

    def to_nb(j):
        return pltpu.make_async_remote_copy(
            sent.at[:, :, :, at_block(j)], dates.at[GAP : GAP + cross, :, :, at_block(j)],
            nb_send.at[j], nb_recv.at[j], device_id=(nb, c), device_id_type=MESH,
        )

    def to_side(side):
        return pltpu.make_async_remote_copy(
            edge.at[side], edge.at[2 + side], edge_send.at[side], edge_recv.at[side],
            device_id=(d, c - 1 if side == 0 else c + 1), device_id_type=MESH,
        )

    def halo_to(which):
        return pltpu.make_async_remote_copy(
            halo, other.at[which], halo_send.at[which], halo_recv.at[which],
            device_id=(sib if which == 0 else nb, c), device_id_type=MESH,
        )

    def results():
        return pltpu.make_async_remote_copy(
            res_far, res_in, res_send, res_recv, device_id=(nb, c), device_id_type=MESH
        )

    def send(j, carry):
        for s in range(cross):
            sent[s, :, :, at_block(j)] = own[sel_out[s], :, :, at_block(j)]

        @pl.when(has_nb)
        def _():
            to_nb(j).start()

        to_sib(j).start()
        return carry

    lax.fori_loop(0, BLOCKS, send, 0)

    lane = lax.broadcasted_iota(jnp.int32, (ROWS, 128), 1)
    left_edge = jnp.zeros((ROWS, 128), F32)
    right_edge = jnp.zeros((ROWS, 128), F32)
    for m in range(2 * GAP):
        tile = pltpu.roll(own[m // 2, m % 2, :, 0:128], 64 + 5 * m, 1)
        left_edge = jnp.where((lane >= 64 + 5 * m) & (lane < 69 + 5 * m), tile, left_edge)
        tile = pltpu.roll(own[m // 2, m % 2, :, WIDTH - 128 : WIDTH], 5 * m + 5, 1)
        right_edge = jnp.where((lane >= 5 * m) & (lane < 5 * m + 5), tile, right_edge)
    edge[0] = left_edge
    edge[1] = right_edge

    @pl.when(has_left)
    def _():
        to_side(0).start()

    @pl.when(has_right)
    def _():
        to_side(1).start()

    def forward_halo():
        @pl.when(has_right)
        def _():
            to_side(0).wait_recv()

        @pl.when(has_left)
        def _():
            to_side(1).wait_recv()

        @pl.when(jnp.logical_not(has_right))
        def _():
            edge[2] = jnp.zeros((ROWS, 128), F32)

        @pl.when(jnp.logical_not(has_left))
        def _():
            edge[3] = jnp.zeros((ROWS, 128), F32)

        halo[...] = jnp.where(lane < 64, edge[3], edge[2])
        halo_to(0).start()

        @pl.when(has_nb)
        def _():
            halo_to(1).start()

    def unpack_halo():
        halo_to(0).wait_recv()

        @pl.when(has_nb)
        def _():
            halo_to(1).wait_recv()

        for source in range(3):
            packed = halo[...] if source == 0 else other[source - 1]
            for m in range(2 * GAP):
                right = pltpu.roll(packed, (54 - 5 * m) % 128, 1)
                left = pltpu.roll(packed, (123 - 5 * m) % 128, 1)
                tile = jnp.where(lane < 123, right, left)
                if source < 2:
                    tiles[GAP * source + m // 2, m % 2] = tile
                else:
                    tiles_nb[m // 2, m % 2] = tile
        for s in range(cross):
            tiles[2 * GAP + s] = tiles_nb[sel_in[s]]

    def windows(par, wrap, at, rows):
        cur, prev = band[2 * wrap], band[2 * wrap + 1]
        total = dot(hi_buf[par, pl.ds(at, rows)], cur) + dot(lo_buf[par, pl.ds(at, rows)], cur)
        total += dot(hi_buf[1 - par, pl.ds(at, rows)], prev)
        return total + dot(lo_buf[1 - par, pl.ds(at, rows)], prev)

    def step(j, tile):
        par = lax.rem(j, 2) if tile else 0
        wrap = jnp.where(j == BLOCKS, 1, 0) if tile else 0
        block = jnp.where(j == BLOCKS, 0, j) if tile else 0

        def arrive():
            to_sib(j).wait_recv()

            @pl.when(has_nb)
            def _():
                to_nb(j).wait_recv()

        if tile:
            pl.when(j < BLOCKS)(arrive)
            pl.when(j == 3)(forward_halo)
            pl.when(j == BLOCKS)(unpack_halo)
        else:
            arrive()

        for date in range(2 * GAP + cross):
            source = own.at[date] if date < GAP else dates.at[date - GAP]
            stage[date] = source[:, :, at_block(block)]

        def power(i, carry):
            if tile:

                @pl.when(j == BLOCKS)
                def _():
                    for e in range(2):
                        for part in range(2):
                            stage[2 * i + e, part, :, 128:256] = jnp.where(
                                lane < 118, stage[2 * i + e, part, :, 128:256], tiles[2 * i + e, part]
                            )

            both = []
            for e in range(2):
                re, im = stage[2 * i + e, 0], stage[2 * i + e, 1]
                both.append(re * re + im * im)
            at = pl.multiple_of(i * (2 * ROWS), 2 * ROWS)
            hi, lo = split(jnp.concatenate(both, axis=0))
            hi_buf[par, pl.ds(at, 2 * ROWS)] = hi
            lo_buf[par, pl.ds(at, 2 * ROWS)] = lo
            if tile:
                total = windows(par, wrap, at, 2 * ROWS)
                for e in range(2):
                    inv[2 * i + e] = lax.rsqrt(row_window(total[e * ROWS : (e + 1) * ROWS]))
            return carry

        lax.fori_loop(0, held // 2, power, 0)

        def pair(r, carry):
            a = jnp.where(r < GAP, r, r + GAP)
            second = [plan[0, 2 * r + q] for q in range(2)]
            re_a, im_a = stage[a, 0], stage[a, 1]
            images = []
            for q in range(2):
                re_b, im_b = stage[second[q], 0], stage[second[q], 1]
                images += [re_a * re_b + im_a * im_b, im_a * re_b - re_a * im_b]
            hi, lo = split(jnp.concatenate(images, axis=0))
            at = pl.multiple_of(power_rows + r * (4 * ROWS), 2 * ROWS)
            hi_buf[par, pl.ds(at, 4 * ROWS)] = hi
            lo_buf[par, pl.ds(at, 4 * ROWS)] = lo

            def looks():
                rows = pl.ds(pl.multiple_of(r * (4 * ROWS), 4 * ROWS), 4 * ROWS)
                acc_ifg[rows] += dot(hi, look_i[j]) + dot(lo, look_i[j])

            if tile:
                pl.when(j < BLOCKS)(looks)
                total = windows(par, wrap, at, 4 * ROWS)
                sums = [row_window(total[f * ROWS : (f + 1) * ROWS]) for f in range(4)]
                inv_a = inv[a]
                coh = []
                for q in range(2):
                    square = sums[2 * q] * sums[2 * q] + sums[2 * q + 1] * sums[2 * q + 1]
                    root = square * lax.rsqrt(jnp.maximum(square, 1e-37))
                    coh.append(root * inv_a * inv[second[q]])
                hi, lo = split(jnp.concatenate(coh, axis=0))
                rows = pl.ds(pl.multiple_of(r * (2 * ROWS), 2 * ROWS), 2 * ROWS)
                acc_coh[rows] += dot(hi, look_c[j]) + dot(lo, look_c[j])
            else:
                looks()
            return carry

        lax.fori_loop(0, starts, pair, 0)

    step(0, False)

    def later(j, carry):
        step(j, True)
        return carry

    lax.fori_loop(1, BLOCKS + 1, later, 0)

    for r in range(starts):
        for q in range(2):
            target = res if r < GAP else res_far
            slot = 2 * r + q if r < GAP else 2 * (r - GAP) + q
            for f in range(3):
                source = acc_ifg if f < 2 else acc_coh
                base = r * 4 * ROWS + (2 * q + f) * ROWS if f < 2 else r * 2 * ROWS + q * ROWS
                total = source[pl.ds(base, 8, stride=5), :]
                for e in range(1, 5):
                    total = total + source[pl.ds(base + e, 8, stride=5), :]
                target[slot, f] = total / 100.0

    @pl.when(has_nb)
    def _():
        results().start()
        results().wait_recv()

    for p in range(2 * GAP):
        here = plan[1, p] == 1
        back = res_in[plan[2, p]]
        value = jnp.where(here, res[p], back)
        out_ifg[p] = value[0:2]
        out_coh[p] = value[2]

    def sent_all(j, carry):
        to_sib(j).wait_send()

        @pl.when(has_nb)
        def _():
            to_nb(j).wait_send()

        return carry

    lax.fori_loop(0, BLOCKS, sent_all, 0)
    halo_to(0).wait_send()

    @pl.when(has_nb)
    def _():
        halo_to(1).wait_send()
        results().wait_send()

    @pl.when(has_left)
    def _():
        to_side(0).wait_send()

    @pl.when(has_right)
    def _():
        to_side(1).wait_send()


def main_call(cross, table, slc):
    starts = GAP + cross
    held = 2 * GAP + cross + cross % 2
    rows = held * ROWS + starts * 4 * ROWS
    vmem, dma = pltpu.VMEM, pltpu.SemaphoreType.DMA
    return pl.pallas_call(
        functools.partial(main_kernel, cross),
        out_shape=(
            jax.ShapeDtypeStruct((2 * GAP, 2, 8, 128), F32),
            jax.ShapeDtypeStruct((2 * GAP, 8, 128), F32),
        ),
        in_specs=[pl.BlockSpec(memory_space=pltpu.SMEM), pl.BlockSpec(memory_space=pl.ANY)],
        out_specs=(pl.BlockSpec(memory_space=vmem), pl.BlockSpec(memory_space=vmem)),
        scratch_shapes=[
            vmem((GAP, 2, ROWS, WIDTH), F32),
            vmem((GAP + cross, 2, ROWS, WIDTH), F32),
            vmem((cross, 2, ROWS, WIDTH), F32),
            vmem((held, 2, ROWS, BLOCK), F32),
            vmem((2, rows, BLOCK), BF16),
            vmem((2, rows, BLOCK), BF16),
            vmem((held, ROWS, BLOCK), F32),
            vmem((starts * 4 * ROWS, 128), F32),
            vmem((starts * 2 * ROWS, 128), F32),
            vmem((BLOCKS + 1, BLOCK, 128), BF16),
            vmem((BLOCKS + 1, BLOCK, 128), BF16),
            vmem((4, BLOCK, BLOCK), BF16),
            vmem((4, ROWS, 128), F32),
            vmem((ROWS, 128), F32),
            vmem((2, ROWS, 128), F32),
            vmem((held, 2, ROWS, 128), F32),
            vmem((GAP, 2, ROWS, 128), F32),
            vmem((2 * GAP, 3, 8, 128), F32),
            vmem((2 * cross, 3, 8, 128), F32),
            vmem((2 * cross, 3, 8, 128), F32),
            pltpu.SMEM((3, 2 * starts), jnp.int32),
            dma,
            dma((BLOCKS,)),
            dma((BLOCKS,)),
            dma((BLOCKS,)),
            dma((BLOCKS,)),
            dma((2,)),
            dma((2,)),
            dma((2,)),
            dma((2,)),
            dma,
            dma,
        ],
        compiler_params=pltpu.CompilerParams(
            collective_id=cross, has_side_effects=True, vmem_limit_bytes=48 * 2**20
        ),
        name="pairs_" + str(cross),
    )(table, slc)


def body(slc, pairs):
    table = pl.pallas_call(
        plan_kernel,
        out_shape=jax.ShapeDtypeStruct((8, 128), jnp.int32),
        in_specs=[pl.BlockSpec(memory_space=pltpu.VMEM)],
        out_specs=pl.BlockSpec(memory_space=pltpu.VMEM),
        name="plan",
    )(pairs)
    return lax.cond(
        table[0, 127] == 0,
        functools.partial(main_call, 2),
        functools.partial(main_call, 3),
        table,
        slc,
    )


def solution(mesh):
    in_specs = (P("date", None, None, "col"), P())
    out_specs = (P("date", None, None, "col"), P("date", None, "col"))
    return jax.shard_map(body, mesh=mesh, in_specs=in_specs, out_specs=out_specs, check_vma=False)
```

```python
import functools

import jax
import jax.numpy as jnp
from jax import lax
from jax.experimental import pallas as pl
from jax.experimental.pallas import tpu as pltpu
from jax.sharding import PartitionSpec as P

GAP = 5
HALF = 5
ROWS = 40
WIDTH = 2560
BLOCK = 256
BLOCKS = WIDTH // BLOCK
LOOK_C = 20
WINDOW = 3
MESH = pl.DeviceIdType.MESH
F32 = jnp.float32
BF16 = jnp.bfloat16


def plan_kernel(pairs_ref, tab_ref):
    rows = pairs_ref.shape[0]
    lane = lax.broadcasted_iota(jnp.int32, (rows, 128), 1)
    row = lax.broadcasted_iota(jnp.int32, (rows, 128), 0)
    second = jnp.broadcast_to(pairs_ref[:, 1:2], (rows, 128))
    lane8 = lax.broadcasted_iota(jnp.int32, (8, 128), 1)
    row8 = lax.broadcasted_iota(jnp.int32, (8, 128), 0)
    sec, dist = [], []
    for q in range(2):
        s = jnp.sum(jnp.where(row == 2 * lane + q, second, 0), axis=0, keepdims=True)
        s = jnp.broadcast_to(s, (8, 128))
        sec.append(s)
        dist.append(jnp.where(lane8 < rows // 2, s - lane8, 0))
    up = jnp.zeros((8, 128), jnp.int32)
    for k in range(1, GAP + 1):
        fwd = jnp.where((dist[0] == k) | (dist[1] == k), 1, 0)
        back = jnp.where((dist[0] == -k) | (dist[1] == -k), 1, 0)
        up = up | ((fwd | pltpu.roll(back, 128 - k, 1)) << (k - 1))
    masks = [pltpu.roll(up, GAP - i, 1) >> (GAP - 1 - i) for i in range(GAP)]
    found = jnp.zeros((8, 128), jnp.int32)
    s0 = jnp.zeros((8, 128), jnp.int32)
    s1 = jnp.ones((8, 128), jnp.int32)
    need = jnp.zeros((8, 128), jnp.int32)
    for lo in range(GAP - 2, -1, -1):
        for hi in range(GAP - 1, lo, -1):
            rest = jnp.zeros((8, 128), jnp.int32)
            for i in range(GAP):
                if i not in (lo, hi):
                    rest = rest | masks[i]
            count = jnp.zeros((8, 128), jnp.int32)
            for j in range(GAP):
                count = count + ((rest >> j) & 1)
            take = (count <= 2) & (found == 0)
            s0 = jnp.where(take, lo, s0)
            s1 = jnp.where(take, hi, s1)
            need = jnp.where(take, rest, need)
            found = jnp.where(take, 1, found)
    t0 = jnp.zeros((8, 128), jnp.int32)
    t1 = jnp.zeros((8, 128), jnp.int32)
    for j in range(GAP):
        t1 = jnp.where(((need >> j) & 1) == 1, j, t1)
        t0 = jnp.where(((need >> (GAP - 1 - j)) & 1) == 1, GAP - 1 - j, t0)
    chip = (lane8 % (2 * GAP) == 0) & (lane8 > 0) & (lane8 < rows // 2)
    missing = jnp.where(chip & (found == 0), 1.0, 0.0)
    wide = jnp.broadcast_to(jnp.max(missing, axis=1, keepdims=True), (8, 128)) > 0.5
    picks = [
        jnp.where(wide, 2, s0),
        jnp.where(wide, 3, s1),
        jnp.where(wide, 4, 0),
        jnp.where(wide, 0, t0),
        jnp.where(wide, 1, t1),
        jnp.zeros((8, 128), jnp.int32),
        sec[0],
        sec[1],
    ]
    table = jnp.zeros((8, 128), jnp.int32)
    for r, value in enumerate(picks):
        table = jnp.where(row8 == r, value, table)
    tab_ref[...] = jnp.where((lane8 == 127) & (row8 == 0), jnp.where(wide, 1, 0), table)


def split(x):
    hi = x.astype(BF16)
    return hi, (x - hi.astype(F32)).astype(BF16)


def row_window(x):
    x = jnp.concatenate([x, jnp.zeros((8, x.shape[1]), F32)], axis=0)
    n = x.shape[0]
    two = x + pltpu.roll(x, n - 1, 0)
    four = two + pltpu.roll(two, n - 2, 0)
    eight = four + pltpu.roll(four, n - 4, 0)
    total = eight + pltpu.roll(two, n - 8, 0) + pltpu.roll(x, n - 10, 0)
    return pltpu.roll(total, HALF, 0)[:ROWS]


def dot(a, b):
    return jnp.dot(a, b, preferred_element_type=F32)


def main_kernel(
    cross, tab, slc, out_ifg, out_coh,
    own, dates, sent, stage, fields, sums, coh, inv, acc_ifg, acc_coh, look_i, look_c, band,
    edge, halo, other, tiles, tiles_nb, res, res_far, res_in, plan,
    load_sem, sib_send, sib_recv, nb_send, nb_recv, edge_send, edge_recv, halo_send, halo_recv, res_send, res_recv,
):
    held = stage.shape[0]
    starts = GAP + cross
    power_rows = held * ROWS
    d, c = lax.axis_index("date"), lax.axis_index("col")
    n_d, n_c = lax.axis_size("date"), lax.axis_size("col")
    odd = lax.rem(d, 2)
    sib = d + 1 - 2 * odd
    nb = d - 1 + 2 * odd
    has_nb = (nb >= 0) & (nb < n_d)
    has_left, has_right = c > 0, c < n_c - 1

    load = pltpu.make_async_copy(slc, own, load_sem)
    load.start()

    barrier = pltpu.get_barrier_semaphore()
    pl.semaphore_signal(barrier, inc=1, device_id=(sib, c), device_id_type=MESH)

    @pl.when(has_nb)
    def _():
        pl.semaphore_signal(barrier, inc=1, device_id=(nb, c), device_id_type=MESH)

    @pl.when(has_left)
    def _():
        pl.semaphore_signal(barrier, inc=1, device_id=(d, c - 1), device_id_type=MESH)

    @pl.when(has_right)
    def _():
        pl.semaphore_signal(barrier, inc=1, device_id=(d, c + 1), device_id_type=MESH)

    lane_of = 5 * (d + odd)
    sel_out = [tab[3 * (1 - odd) + s, lane_of] for s in range(cross)]
    sel_in = [tab[3 * odd + s, lane_of] for s in range(cross)]
    for r in range(GAP):
        for q in range(2):
            b = tab[6 + q, GAP * d + r]
            mine, sibling, far = b - GAP * d, b - GAP * sib, b - GAP * nb
            in_own = (mine >= 0) & (mine < GAP)
            in_sib = (sibling >= 0) & (sibling < GAP)
            place, here, back = jnp.int32(0), jnp.int32(0), jnp.int32(0)
            for s in range(cross):
                match = has_nb & (sel_in[s] == far)
                place = jnp.where(match, 2 * GAP + s, place)
                here = jnp.where(match, 1, here)
                back = jnp.where(sel_out[s] == r, 2 * s + q, back)
            place = jnp.where(in_own, mine, jnp.where(in_sib, GAP + sibling, place))
            here = jnp.where(in_own | in_sib, 1, here)
            plan[0, 2 * r + q] = place
            plan[1, 2 * r + q] = here
            plan[2, 2 * r + q] = back
    for s in range(cross):
        for q in range(2):
            far_date = jnp.clip(GAP * nb + sel_in[s], 0, GAP * n_d - 1)
            mine = tab[6 + q, far_date] - GAP * d
            plan[0, 2 * (GAP + s) + q] = jnp.where((mine >= 0) & (mine < GAP), mine, 0)

    k = lax.broadcasted_iota(jnp.int32, (BLOCK, BLOCK), 0)
    n = lax.broadcasted_iota(jnp.int32, (BLOCK, BLOCK), 1)
    near = lambda x: jnp.abs(x) <= HALF
    left_half = n < BLOCK // 2
    wrapped = jnp.where(
        left_half,
        jnp.where((k >= 246) & (k < 251) & near(k - 246 - (n - 128)), 1.0, 0.0),
        jnp.where(((k < 246) & near(k - n + 128)) | ((k >= 251) & near(k - 256 - n + 128)), 1.0, 0.0),
    )
    matrices = [
        jnp.where(near(k - n + 128), 1.0, 0.0),
        jnp.where(near(k - n - 128), 1.0, 0.0),
        wrapped,
        jnp.where(left_half & near(k - n - 128), 1.0, 0.0),
    ]
    for variant, order in enumerate(((0, 1), (1, 0), (2, 3))):
        for e in range(4):
            band[variant, e * BLOCK : (e + 1) * BLOCK] = matrices[order[e // 2]].astype(BF16)

    def fill_look(j, carry):
        column = lax.broadcasted_iota(jnp.int32, (BLOCK, 128), 0) + j * BLOCK
        first = lax.broadcasted_iota(jnp.int32, (BLOCK, 128), 1) * LOOK_C
        at = column - first
        ifg = jnp.where((at >= 0) & (at < LOOK_C), 1.0, 0.0).astype(BF16)
        at = column - BLOCK // 2
        at = jnp.where(at >= WIDTH, at - WIDTH, at) - first
        shifted = jnp.where((at >= 0) & (at < LOOK_C), 1.0, 0.0).astype(BF16)
        for e in range(2):
            look_i[j, e * BLOCK : (e + 1) * BLOCK] = ifg
            look_c[j, e * BLOCK : (e + 1) * BLOCK] = shifted
        return carry

    lax.fori_loop(0, BLOCKS + 1, fill_look, 0)
    acc_ifg[...] = jnp.zeros_like(acc_ifg)
    acc_coh[...] = jnp.zeros_like(acc_coh)

    @pl.when(jnp.logical_not(has_nb))
    def _():
        dates[GAP : GAP + cross] = jnp.zeros((cross, 2, ROWS, WIDTH), F32)
        other[1] = jnp.zeros((ROWS, 128), F32)
        res_in[...] = jnp.zeros_like(res_in)

    if held > 2 * GAP + cross:
        stage[held - 1] = jnp.zeros((2, ROWS, BLOCK), F32)
        tiles[held - 1] = jnp.zeros((2, ROWS, 128), F32)

    pl.semaphore_wait(
        barrier, 1 + has_nb.astype(jnp.int32) + has_left.astype(jnp.int32) + has_right.astype(jnp.int32)
    )
    load.wait()

    def at_block(j):
        return pl.ds(pl.multiple_of(j * BLOCK, BLOCK), BLOCK)

    def to_sib(j):
        return pltpu.make_async_remote_copy(
            own.at[:, :, :, at_block(j)], dates.at[0:GAP, :, :, at_block(j)],
            sib_send.at[j], sib_recv.at[j], device_id=(sib, c), device_id_type=MESH,
        )

    def to_nb(j):
        return pltpu.make_async_remote_copy(
            sent.at[:, :, :, at_block(j)], dates.at[GAP : GAP + cross, :, :, at_block(j)],
            nb_send.at[j], nb_recv.at[j], device_id=(nb, c), device_id_type=MESH,
        )

    def to_side(side):
        return pltpu.make_async_remote_copy(
            edge.at[side], edge.at[2 + side], edge_send.at[side], edge_recv.at[side],
            device_id=(d, c - 1 if side == 0 else c + 1), device_id_type=MESH,
        )

    def halo_to(which):
        return pltpu.make_async_remote_copy(
            halo, other.at[which], halo_send.at[which], halo_recv.at[which],
            device_id=(sib if which == 0 else nb, c), device_id_type=MESH,
        )

    def results():
        return pltpu.make_async_remote_copy(
            res_far, res_in, res_send, res_recv, device_id=(nb, c), device_id_type=MESH
        )

    def send(j, carry):
        for s in range(cross):
            sent[s, :, :, at_block(j)] = own[sel_out[s], :, :, at_block(j)]

        @pl.when(has_nb & (j < (WINDOW or BLOCKS)))
        def _():
            to_nb(j).start()

        to_sib(j).start()
        return carry

    lax.fori_loop(0, BLOCKS, send, 0)

    lane = lax.broadcasted_iota(jnp.int32, (ROWS, 128), 1)
    left_edge = jnp.zeros((ROWS, 128), F32)
    right_edge = jnp.zeros((ROWS, 128), F32)
    for m in range(2 * GAP):
        tile = pltpu.roll(own[m // 2, m % 2, :, 0:128], 64 + 5 * m, 1)
        left_edge = jnp.where((lane >= 64 + 5 * m) & (lane < 69 + 5 * m), tile, left_edge)
        tile = pltpu.roll(own[m // 2, m % 2, :, WIDTH - 128 : WIDTH], 5 * m + 5, 1)
        right_edge = jnp.where((lane >= 5 * m) & (lane < 5 * m + 5), tile, right_edge)
    edge[0] = left_edge
    edge[1] = right_edge

    @pl.when(has_left)
    def _():
        to_side(0).start()

    @pl.when(has_right)
    def _():
        to_side(1).start()

    def forward_halo():
        @pl.when(has_right)
        def _():
            to_side(0).wait_recv()

        @pl.when(has_left)
        def _():
            to_side(1).wait_recv()

        @pl.when(jnp.logical_not(has_right))
        def _():
            edge[2] = jnp.zeros((ROWS, 128), F32)

        @pl.when(jnp.logical_not(has_left))
        def _():
            edge[3] = jnp.zeros((ROWS, 128), F32)

        halo[...] = jnp.where(lane < 64, edge[3], edge[2])
        halo_to(0).start()

        @pl.when(has_nb)
        def _():
            halo_to(1).start()

    def unpack_halo():
        halo_to(0).wait_recv()

        @pl.when(has_nb)
        def _():
            halo_to(1).wait_recv()

        for source in range(3):
            packed = halo[...] if source == 0 else other[source - 1]
            for m in range(2 * GAP):
                right = pltpu.roll(packed, (54 - 5 * m) % 128, 1)
                left = pltpu.roll(packed, (123 - 5 * m) % 128, 1)
                tile = jnp.where(lane < 123, right, left)
                if source < 2:
                    tiles[GAP * source + m // 2, m % 2] = tile
                else:
                    tiles_nb[m // 2, m % 2] = tile
        for s in range(cross):
            tiles[2 * GAP + s] = tiles_nb[sel_in[s]]

    def keep_split(target, rows, x, par=0):
        hi, lo = split(x)
        target[rows, pl.ds(pl.multiple_of(par * 2 * BLOCK, BLOCK), BLOCK)] = hi
        target[rows, pl.ds(pl.multiple_of(par * 2 * BLOCK + BLOCK, BLOCK), BLOCK)] = lo

    def step(j, tile):
        par = lax.rem(j, 2) if tile else 0
        wrap = jnp.where(j == BLOCKS, 1, 0) if tile else 0
        block = jnp.where(j == BLOCKS, 0, j) if tile else 0

        def arrive():
            to_sib(j).wait_recv()

            @pl.when(has_nb)
            def _():
                to_nb(j).wait_recv()

        if tile:
            pl.when(j < BLOCKS)(arrive)
            pl.when(j == 3)(forward_halo)
            pl.when(j == BLOCKS)(unpack_halo)
        else:
            arrive()

        for date in range(2 * GAP + cross):
            source = own.at[date] if date < GAP else dates.at[date - GAP]
            stage[date] = source[:, :, at_block(block)]
        if tile:

            @pl.when(j == BLOCKS)
            def _():
                for date in range(held):
                    for part in range(2):
                        stage[date, part, :, 128:256] = jnp.where(
                            lane < 118, stage[date, part, :, 128:256], tiles[date, part]
                        )

        if WINDOW:

            @pl.when(j + WINDOW < BLOCKS)
            def _():
                @pl.when(has_nb)
                def _():
                    to_nb(j).wait_send()
                    to_nb(j + WINDOW).start()

        def power(i, carry):
            both = []
            for e in range(2):
                re, im = stage[2 * i + e, 0], stage[2 * i + e, 1]
                both.append(re * re + im * im)
            at = pl.multiple_of(i * (2 * ROWS), 2 * ROWS)
            keep_split(fields, pl.ds(at, 2 * ROWS), jnp.concatenate(both, axis=0), par)
            return carry

        lax.fori_loop(0, held // 2, power, 0)

        def product(r, carry):
            a = jnp.where(r < GAP, r, r + GAP)
            re_a, im_a = stage[a, 0], stage[a, 1]
            images = []
            for q in range(2):
                b = plan[0, 2 * r + q]
                re_b, im_b = stage[b, 0], stage[b, 1]
                images += [re_a * re_b + im_a * im_b, im_a * re_b - re_a * im_b]
            at = pl.multiple_of(power_rows + r * (4 * ROWS), 2 * ROWS)
            keep_split(fields, pl.ds(at, 4 * ROWS), jnp.concatenate(images, axis=0), par)
            return carry

        lax.fori_loop(0, starts, product, 0)

        def looks():
            half = pl.ds(pl.multiple_of(par * 2 * BLOCK, 2 * BLOCK), 2 * BLOCK)
            acc_ifg[...] += dot(fields[power_rows:, half], look_i[j])

        if not tile:
            looks()
            return
        pl.when(j < BLOCKS)(looks)
        sums[...] = dot(fields[...], band[par + 2 * wrap])

        def root(i, carry):
            for e in range(2):
                at = pl.multiple_of(i * (2 * ROWS) + e * ROWS, ROWS)
                inv[2 * i + e] = lax.rsqrt(row_window(sums[pl.ds(at, ROWS)]))
            return carry

        lax.fori_loop(0, held // 2, root, 0)

        def ratio(r, carry):
            at = power_rows + r * (4 * ROWS)
            part = [row_window(sums[pl.ds(pl.multiple_of(at + f * ROWS, ROWS), ROWS)]) for f in range(4)]
            inv_a = inv[jnp.where(r < GAP, r, r + GAP)]
            both = []
            for q in range(2):
                square = part[2 * q] * part[2 * q] + part[2 * q + 1] * part[2 * q + 1]
                size = square * lax.rsqrt(jnp.maximum(square, 1e-37))
                both.append(size * inv_a * inv[plan[0, 2 * r + q]])
            at = pl.multiple_of(r * (2 * ROWS), 2 * ROWS)
            keep_split(coh, pl.ds(at, 2 * ROWS), jnp.concatenate(both, axis=0))
            return carry

        lax.fori_loop(0, starts, ratio, 0)
        acc_coh[...] += dot(coh[...], look_c[j])

    step(0, False)

    def later(j, carry):
        step(j, True)
        return carry

    lax.fori_loop(1, BLOCKS + 1, later, 0)

    for r in range(starts):
        for q in range(2):
            target = res if r < GAP else res_far
            slot = 2 * r + q if r < GAP else 2 * (r - GAP) + q
            for f in range(3):
                source = acc_ifg if f < 2 else acc_coh
                base = r * 4 * ROWS + (2 * q + f) * ROWS if f < 2 else r * 2 * ROWS + q * ROWS
                total = source[pl.ds(base, 8, stride=5), :]
                for e in range(1, 5):
                    total = total + source[pl.ds(base + e, 8, stride=5), :]
                target[slot, f] = total / 100.0

    @pl.when(has_nb)
    def _():
        results().start()
        results().wait_recv()

    for p in range(2 * GAP):
        here = plan[1, p] == 1
        back = res_in[plan[2, p]]
        value = jnp.where(here, res[p], back)
        out_ifg[p] = value[0:2]
        out_coh[p] = value[2]

    def sent_all(j, carry):
        to_sib(j).wait_send()

        @pl.when(has_nb & (j >= (BLOCKS - WINDOW if WINDOW else 0)))
        def _():
            to_nb(j).wait_send()

        return carry

    lax.fori_loop(0, BLOCKS, sent_all, 0)
    halo_to(0).wait_send()

    @pl.when(has_nb)
    def _():
        halo_to(1).wait_send()
        results().wait_send()

    @pl.when(has_left)
    def _():
        to_side(0).wait_send()

    @pl.when(has_right)
    def _():
        to_side(1).wait_send()


def main_call(cross, table, slc):
    starts = GAP + cross
    held = 2 * GAP + cross + cross % 2
    rows = held * ROWS + starts * 4 * ROWS
    vmem, dma = pltpu.VMEM, pltpu.SemaphoreType.DMA
    return pl.pallas_call(
        functools.partial(main_kernel, cross),
        out_shape=(
            jax.ShapeDtypeStruct((2 * GAP, 2, 8, 128), F32),
            jax.ShapeDtypeStruct((2 * GAP, 8, 128), F32),
        ),
        in_specs=[pl.BlockSpec(memory_space=pltpu.SMEM), pl.BlockSpec(memory_space=pl.ANY)],
        out_specs=(pl.BlockSpec(memory_space=vmem), pl.BlockSpec(memory_space=vmem)),
        scratch_shapes=[
            vmem((GAP, 2, ROWS, WIDTH), F32),
            vmem((GAP + cross, 2, ROWS, WIDTH), F32),
            vmem((cross, 2, ROWS, WIDTH), F32),
            vmem((held, 2, ROWS, BLOCK), F32),
            vmem((rows, 4 * BLOCK), BF16),
            vmem((rows, BLOCK), F32),
            vmem((starts * 2 * ROWS, 2 * BLOCK), BF16),
            vmem((held, ROWS, BLOCK), F32),
            vmem((starts * 4 * ROWS, 128), F32),
            vmem((starts * 2 * ROWS, 128), F32),
            vmem((BLOCKS + 1, 2 * BLOCK, 128), BF16),
            vmem((BLOCKS + 1, 2 * BLOCK, 128), BF16),
            vmem((3, 4 * BLOCK, BLOCK), BF16),
            vmem((4, ROWS, 128), F32),
            vmem((ROWS, 128), F32),
            vmem((2, ROWS, 128), F32),
            vmem((held, 2, ROWS, 128), F32),
            vmem((GAP, 2, ROWS, 128), F32),
            vmem((2 * GAP, 3, 8, 128), F32),
            vmem((2 * cross, 3, 8, 128), F32),
            vmem((2 * cross, 3, 8, 128), F32),
            pltpu.SMEM((3, 2 * starts), jnp.int32),
            dma,
            dma((BLOCKS,)),
            dma((BLOCKS,)),
            dma((BLOCKS,)),
            dma((BLOCKS,)),
            dma((2,)),
            dma((2,)),
            dma((2,)),
            dma((2,)),
            dma,
            dma,
        ],
        compiler_params=pltpu.CompilerParams(
            collective_id=cross, has_side_effects=True, vmem_limit_bytes=48 * 2**20
        ),
        name="pairs_" + str(cross),
    )(table, slc)


def body(slc, pairs):
    table = pl.pallas_call(
        plan_kernel,
        out_shape=jax.ShapeDtypeStruct((8, 128), jnp.int32),
        in_specs=[pl.BlockSpec(memory_space=pltpu.VMEM)],
        out_specs=pl.BlockSpec(memory_space=pltpu.VMEM),
        name="plan",
    )(pairs)
    return lax.cond(
        table[0, 127] == 0,
        functools.partial(main_call, 2),
        functools.partial(main_call, 3),
        table,
        slc,
    )


def solution(mesh):
    in_specs = (P("date", None, None, "col"), P())
    out_specs = (P("date", None, None, "col"), P("date", None, "col"))
    return jax.shard_map(body, mesh=mesh, in_specs=in_specs, out_specs=out_specs, check_vma=False)
```

```python
import functools

import jax
import jax.numpy as jnp
from jax import lax
from jax.experimental import pallas as pl
from jax.experimental.pallas import tpu as pltpu
from jax.sharding import PartitionSpec as P

GAP = 5
HALF = 5
ROWS = 40
WIDTH = 2560
BLOCK = 256
BLOCKS = WIDTH // BLOCK
LOOK_C = 20
WINDOW = 3
MESH = pl.DeviceIdType.MESH
F32 = jnp.float32
BF16 = jnp.bfloat16


def plan_kernel(pairs_ref, tab_ref):
    rows = pairs_ref.shape[1]
    lane = lax.broadcasted_iota(jnp.int32, (rows, 128), 1)
    row = lax.broadcasted_iota(jnp.int32, (rows, 128), 0)
    second = jnp.broadcast_to(pairs_ref[1:2, :], (8, rows)).astype(F32).astype(BF16)
    lane8 = lax.broadcasted_iota(jnp.int32, (8, 128), 1)
    row8 = lax.broadcasted_iota(jnp.int32, (8, 128), 0)
    sec, dist = [], []
    for q in range(2):
        pick = jnp.where(row == 2 * lane + q, 1.0, 0.0).astype(BF16)
        s = dot(second, pick).astype(jnp.int32)
        sec.append(s)
        dist.append(jnp.where(lane8 < rows // 2, s - lane8, 0))
    up = jnp.zeros((8, 128), jnp.int32)
    for k in range(1, GAP + 1):
        fwd = jnp.where((dist[0] == k) | (dist[1] == k), 1, 0)
        back = jnp.where((dist[0] == -k) | (dist[1] == -k), 1, 0)
        up = up | ((fwd | pltpu.roll(back, 128 - k, 1)) << (k - 1))
    masks = [pltpu.roll(up, GAP - i, 1) >> (GAP - 1 - i) for i in range(GAP)]
    found = jnp.zeros((8, 128), jnp.int32)
    s0 = jnp.zeros((8, 128), jnp.int32)
    s1 = jnp.ones((8, 128), jnp.int32)
    need = jnp.zeros((8, 128), jnp.int32)
    for lo in range(GAP - 2, -1, -1):
        for hi in range(GAP - 1, lo, -1):
            rest = jnp.zeros((8, 128), jnp.int32)
            for i in range(GAP):
                if i not in (lo, hi):
                    rest = rest | masks[i]
            count = jnp.zeros((8, 128), jnp.int32)
            for j in range(GAP):
                count = count + ((rest >> j) & 1)
            take = (count <= 2) & (found == 0)
            s0 = jnp.where(take, lo, s0)
            s1 = jnp.where(take, hi, s1)
            need = jnp.where(take, rest, need)
            found = jnp.where(take, 1, found)
    t0 = jnp.zeros((8, 128), jnp.int32)
    t1 = jnp.zeros((8, 128), jnp.int32)
    for j in range(GAP):
        t1 = jnp.where(((need >> j) & 1) == 1, j, t1)
        t0 = jnp.where(((need >> (GAP - 1 - j)) & 1) == 1, GAP - 1 - j, t0)
    chip = (lane8 % (2 * GAP) == 0) & (lane8 > 0) & (lane8 < rows // 2)
    missing = jnp.where(chip & (found == 0), 1.0, 0.0)
    wide = jnp.broadcast_to(jnp.max(missing, axis=1, keepdims=True), (8, 128)) > 0.5
    picks = [
        jnp.where(wide, 2, s0),
        jnp.where(wide, 3, s1),
        jnp.where(wide, 4, 0),
        jnp.where(wide, 0, t0),
        jnp.where(wide, 1, t1),
        jnp.zeros((8, 128), jnp.int32),
        sec[0],
        sec[1],
    ]
    table = jnp.zeros((8, 128), jnp.int32)
    for r, value in enumerate(picks):
        table = jnp.where(row8 == r, value, table)
    tab_ref[...] = jnp.where((lane8 == 127) & (row8 == 0), jnp.where(wide, 1, 0), table)


def split(x):
    hi = x.astype(BF16)
    return hi, (x - hi.astype(F32)).astype(BF16)


def dot(a, b):
    return jnp.dot(a, b, preferred_element_type=F32)


def main_kernel(
    cross, tab, slc, out_ifg, out_coh,
    own, dates, sent, stage, fields, sums, image, ratio, look_rows, inv, acc_ifg, acc_coh, look_i, look_c, band,
    relayed, edge, halo, other, tiles, tiles_nb, res, res_far, res_in, plan,
    load_sem, sib_send, sib_recv, nb_send, nb_recv, edge_send, edge_recv, halo_send, halo_recv, res_send, res_recv,
    relay_send, relay_recv,
):
    held = stage.shape[0]
    starts = GAP + cross
    power_rows = held * ROWS
    d, c = lax.axis_index("date"), lax.axis_index("col")
    n_d, n_c = lax.axis_size("date"), lax.axis_size("col")
    odd = lax.rem(d, 2)
    sib = d + 1 - 2 * odd
    nb = d - 1 + 2 * odd
    has_nb = (nb >= 0) & (nb < n_d)
    has_left, has_right = c > 0, c < n_c - 1

    kind = lax.rem(d, 4)
    onward = kind % 2 == 1
    relay_by = jnp.where(onward, d + 3, d - 3)
    relay_to = jnp.where(kind < 2, d + 2, d - 2)
    shared = (relay_by >= 0) & (relay_by < n_d)
    is_relay = shared & ((kind == 1) | (kind == 2))
    is_end = shared & ((kind == 0) | (kind == 3))
    line = lax.div(d, 4) - jnp.where(onward, 0, 1)
    share = jnp.where(kind >= 2, line, 2 - line)

    def by_relay(j):
        few = (j == 1) | (j == 4) | (j == 6)
        half = (j == 0) | (j == 2) | (j == 4) | (j == 5) | (j == 7)
        most = (j < 8) & (j != 4)
        return ((share == 0) & few) | ((share == 1) & half) | ((share == 2) & most)

    load = pltpu.make_async_copy(slc, own, load_sem)
    load.start()

    barrier = pltpu.get_barrier_semaphore()
    pl.semaphore_signal(barrier, inc=1, device_id=(sib, c), device_id_type=MESH)

    @pl.when(has_nb)
    def _():
        pl.semaphore_signal(barrier, inc=1, device_id=(nb, c), device_id_type=MESH)

    @pl.when(shared)
    def _():
        pl.semaphore_signal(barrier, inc=1, device_id=(relay_by, c), device_id_type=MESH)
        pl.semaphore_signal(barrier, inc=1, device_id=(relay_to, c), device_id_type=MESH)

    @pl.when(has_left)
    def _():
        pl.semaphore_signal(barrier, inc=1, device_id=(d, c - 1), device_id_type=MESH)

    @pl.when(has_right)
    def _():
        pl.semaphore_signal(barrier, inc=1, device_id=(d, c + 1), device_id_type=MESH)

    lane_of = 5 * (d + odd)
    sel_out = [tab[3 * (1 - odd) + s, lane_of] for s in range(cross)]
    sel_in = [tab[3 * odd + s, lane_of] for s in range(cross)]
    greeted = 1 + jnp.where(has_nb, 1, 0) + jnp.where(has_left, 1, 0) + jnp.where(has_right, 1, 0)
    pl.semaphore_wait(barrier, greeted + jnp.where(shared, 2, 0))
    load.wait()

    def at_block(j):
        return pl.ds(pl.multiple_of(j * BLOCK, BLOCK), BLOCK)

    def to_sib(j):
        return pltpu.make_async_remote_copy(
            own.at[:, :, :, at_block(j)], dates.at[0:GAP, :, :, at_block(j)],
            sib_send.at[j], sib_recv.at[j], device_id=(sib, c), device_id_type=MESH,
        )

    def to_nb(j):
        return pltpu.make_async_remote_copy(
            sent.at[:, :, :, at_block(j)], dates.at[GAP : GAP + cross, :, :, at_block(j)],
            nb_send.at[j], nb_recv.at[j], device_id=(nb, c), device_id_type=MESH,
        )

    def to_relay(j):
        return pltpu.make_async_remote_copy(
            sent.at[:, :, :, at_block(j)], relayed.at[:, :, :, at_block(j)],
            nb_send.at[j], relay_recv.at[j], device_id=(relay_by, c), device_id_type=MESH,
        )

    def relay(j):
        return pltpu.make_async_remote_copy(
            relayed.at[:, :, :, at_block(j)], dates.at[GAP : GAP + cross, :, :, at_block(j)],
            relay_send.at[j], nb_recv.at[j], device_id=(relay_to, c), device_id_type=MESH,
        )

    def start_out(j):
        around = is_end & by_relay(j)

        @pl.when(has_nb & jnp.logical_not(around))
        def _():
            to_nb(j).start()

        @pl.when(around)
        def _():
            to_relay(j).start()

    def pass_on(j):
        @pl.when(is_relay & by_relay(j))
        def _():
            to_relay(j).wait_recv()
            relay(j).start()

    def to_side(side):
        return pltpu.make_async_remote_copy(
            edge.at[side], edge.at[2 + side], edge_send.at[side], edge_recv.at[side],
            device_id=(d, c - 1 if side == 0 else c + 1), device_id_type=MESH,
        )

    def halo_to(which):
        return pltpu.make_async_remote_copy(
            halo, other.at[which], halo_send.at[which], halo_recv.at[which],
            device_id=(sib if which == 0 else nb, c), device_id_type=MESH,
        )

    def results():
        return pltpu.make_async_remote_copy(
            res_far, res_in, res_send, res_recv, device_id=(nb, c), device_id_type=MESH
        )

    def send(j, carry):
        for s in range(cross):
            sent[s, :, :, at_block(j)] = own[sel_out[s], :, :, at_block(j)]

        pl.when(j < WINDOW)(lambda: start_out(j))
        to_sib(j).start()
        return carry

    lax.fori_loop(0, BLOCKS, send, 0)

    for r in range(GAP):
        for q in range(2):
            b = tab[6 + q, GAP * d + r]
            mine, sibling, far = b - GAP * d, b - GAP * sib, b - GAP * nb
            in_own = (mine >= 0) & (mine < GAP)
            in_sib = (sibling >= 0) & (sibling < GAP)
            place, here, back = jnp.int32(0), jnp.int32(0), jnp.int32(0)
            for s in range(cross):
                match = has_nb & (sel_in[s] == far)
                place = jnp.where(match, 2 * GAP + s, place)
                here = jnp.where(match, 1, here)
                back = jnp.where(sel_out[s] == r, 2 * s + q, back)
            place = jnp.where(in_own, mine, jnp.where(in_sib, GAP + sibling, place))
            here = jnp.where(in_own | in_sib, 1, here)
            plan[0, 2 * r + q] = place
            plan[1, 2 * r + q] = here
            plan[2, 2 * r + q] = back
    for s in range(cross):
        for q in range(2):
            far_date = jnp.clip(GAP * nb + sel_in[s], 0, GAP * n_d - 1)
            mine = tab[6 + q, far_date] - GAP * d
            plan[0, 2 * (GAP + s) + q] = jnp.where((mine >= 0) & (mine < GAP), mine, 0)

    k = lax.broadcasted_iota(jnp.int32, (BLOCK, BLOCK), 0)
    n = lax.broadcasted_iota(jnp.int32, (BLOCK, BLOCK), 1)
    near = lambda x: jnp.abs(x) <= HALF
    left_half = n < BLOCK // 2
    wrapped = jnp.where(
        left_half,
        jnp.where((k >= 246) & (k < 251) & near(k - 246 - (n - 128)), 1.0, 0.0),
        jnp.where(((k < 246) & near(k - n + 128)) | ((k >= 251) & near(k - 256 - n + 128)), 1.0, 0.0),
    )
    matrices = [
        jnp.where(near(k - n + 128), 1.0, 0.0),
        jnp.where(near(k - n - 128), 1.0, 0.0),
        wrapped,
        jnp.where(left_half & near(k - n - 128), 1.0, 0.0),
    ]
    for variant, order in enumerate(((0, 1), (1, 0), (2, 3))):
        for e in range(4):
            band[variant, e * BLOCK : (e + 1) * BLOCK] = matrices[order[e // 2]].astype(BF16)

    def fill_look(j, carry):
        column = lax.broadcasted_iota(jnp.int32, (BLOCK, 128), 0) + j * BLOCK
        first = lax.broadcasted_iota(jnp.int32, (BLOCK, 128), 1) * LOOK_C
        at = column - first
        ifg = jnp.where((at >= 0) & (at < LOOK_C), 1.0, 0.0).astype(BF16)
        at = column - BLOCK // 2
        at = jnp.where(at >= WIDTH, at - WIDTH, at) - first
        shifted = jnp.where((at >= 0) & (at < LOOK_C), 1.0, 0.0).astype(BF16)
        for e in range(2):
            look_i[j, e * BLOCK : (e + 1) * BLOCK] = ifg
            look_c[j, e * BLOCK : (e + 1) * BLOCK] = shifted
        return carry

    lax.fori_loop(0, BLOCKS + 1, fill_look, 0)
    acc_ifg[...] = jnp.zeros_like(acc_ifg)
    acc_coh[...] = jnp.zeros_like(acc_coh)
    ratio[...] = jnp.zeros_like(ratio)
    sums[:, :, 0:8] = jnp.zeros((sums.shape[0], 2, 8, 128), F32)
    sums[:, :, 48:56] = jnp.zeros((sums.shape[0], 2, 8, 128), F32)

    @pl.when(jnp.logical_not(has_nb))
    def _():
        dates[GAP : GAP + cross] = jnp.zeros((cross, 2, ROWS, WIDTH), F32)
        other[1] = jnp.zeros((ROWS, 128), F32)
        res_in[...] = jnp.zeros_like(res_in)

    if held > 2 * GAP + cross:
        stage[held - 1] = jnp.zeros((2, ROWS, BLOCK), F32)
        tiles[held - 1] = jnp.zeros((2, ROWS, 128), F32)


    lane = lax.broadcasted_iota(jnp.int32, (ROWS, 128), 1)
    left_edge = jnp.zeros((ROWS, 128), F32)
    right_edge = jnp.zeros((ROWS, 128), F32)
    for m in range(2 * GAP):
        tile = pltpu.roll(own[m // 2, m % 2, :, 0:128], 64 + 5 * m, 1)
        left_edge = jnp.where((lane >= 64 + 5 * m) & (lane < 69 + 5 * m), tile, left_edge)
        tile = pltpu.roll(own[m // 2, m % 2, :, WIDTH - 128 : WIDTH], 5 * m + 5, 1)
        right_edge = jnp.where((lane >= 5 * m) & (lane < 5 * m + 5), tile, right_edge)
    edge[0] = left_edge
    edge[1] = right_edge

    @pl.when(has_left)
    def _():
        to_side(0).start()

    @pl.when(has_right)
    def _():
        to_side(1).start()

    def forward_halo():
        @pl.when(has_right)
        def _():
            to_side(0).wait_recv()

        @pl.when(has_left)
        def _():
            to_side(1).wait_recv()

        @pl.when(jnp.logical_not(has_right))
        def _():
            edge[2] = jnp.zeros((ROWS, 128), F32)

        @pl.when(jnp.logical_not(has_left))
        def _():
            edge[3] = jnp.zeros((ROWS, 128), F32)

        halo[...] = jnp.where(lane < 64, edge[3], edge[2])
        halo_to(0).start()

        @pl.when(has_nb)
        def _():
            halo_to(1).start()

    def unpack_halo():
        halo_to(0).wait_recv()

        @pl.when(has_nb)
        def _():
            halo_to(1).wait_recv()

        for source in range(3):
            packed = halo[...] if source == 0 else other[source - 1]
            for m in range(2 * GAP):
                right = pltpu.roll(packed, (54 - 5 * m) % 128, 1)
                left = pltpu.roll(packed, (123 - 5 * m) % 128, 1)
                tile = jnp.where(lane < 123, right, left)
                if source < 2:
                    tiles[GAP * source + m // 2, m % 2] = tile
                else:
                    tiles_nb[m // 2, m % 2] = tile
        for s in range(cross):
            tiles[2 * GAP + s] = tiles_nb[sel_in[s]]

    def keep_split(target, rows, x, par=0):
        hi, lo = split(x)
        target[rows, pl.ds(pl.multiple_of(par * 2 * BLOCK, BLOCK), BLOCK)] = hi
        target[rows, pl.ds(pl.multiple_of(par * 2 * BLOCK + BLOCK, BLOCK), BLOCK)] = lo

    def row_window(f):
        halves = []
        for h in range(2):
            total = None
            for o in range(3, 11):
                if o < 6:
                    x = sums[f, h, o : o + 48]
                    x = x[0:ROWS] + x[8:48]
                else:
                    x = sums[f, h, o : o + ROWS]
                total = x if total is None else total + x
            halves.append(total)
        return jnp.concatenate(halves, axis=1)

    def keep(target, f, x):
        for h in range(2):
            target[f, h] = x[:, h * 128 : (h + 1) * 128]

    def add_looks(acc, source, look, count):
        def rows(i, carry):
            fields_of = []
            for e in range(4):
                halves = []
                for h in range(2):
                    total = source[4 * i + e, h, pl.ds(0, 8, stride=5), :]
                    for o in range(1, 5):
                        total = total + source[4 * i + e, h, pl.ds(o, 8, stride=5), :]
                    halves.append(total)
                fields_of.append(jnp.concatenate(halves, axis=1))
            at = pl.multiple_of(i * 32, 32)
            keep_split(look_rows, pl.ds(at, 32), jnp.concatenate(fields_of, axis=0))
            return carry

        lax.fori_loop(0, count // 4, rows, 0, unroll=True)
        acc[...] += dot(look_rows[0 : 8 * count], look)

    def step(j, tile):
        par = lax.rem(j, 2) if tile else 0
        wrap = jnp.where(j == BLOCKS, 1, 0) if tile else 0
        block = jnp.where(j == BLOCKS, 0, j) if tile else 0

        def arrive():
            to_sib(j).wait_recv()

            @pl.when(has_nb)
            def _():
                to_nb(j).wait_recv()

        if tile:
            pl.when(j + 1 < BLOCKS)(lambda: pass_on(j + 1))
            pl.when(j < BLOCKS)(arrive)
            pl.when(j == 2)(forward_halo)
            pl.when(j == 6)(unpack_halo)
        else:
            pass_on(0)
            pass_on(1)
            arrive()

        for date in range(2 * GAP + cross):
            source = own.at[date] if date < GAP else dates.at[date - GAP]
            stage[date] = source[:, :, at_block(block)]
        if tile:

            @pl.when(j == BLOCKS)
            def _():
                for date in range(held):
                    for part in range(2):
                        stage[date, part, :, 128:256] = jnp.where(
                            lane < 118, stage[date, part, :, 128:256], tiles[date, part]
                        )

        @pl.when(j + WINDOW < BLOCKS)
        def _():
            @pl.when(has_nb)
            def _():
                to_nb(j).wait_send()

            start_out(j + WINDOW)

        def power(i, carry):
            both = []
            for e in range(2):
                re, im = stage[2 * i + e, 0], stage[2 * i + e, 1]
                both.append(re * re + im * im)
            at = pl.multiple_of(i * (2 * ROWS), 2 * ROWS)
            keep_split(fields, pl.ds(at, 2 * ROWS), jnp.concatenate(both, axis=0), par)
            return carry

        lax.fori_loop(0, held // 2, power, 0)

        def product(r, carry):
            a = jnp.where(r < GAP, r, r + GAP)
            re_a, im_a = stage[a, 0], stage[a, 1]
            images = []
            for q in range(2):
                b = plan[0, 2 * r + q]
                re_b, im_b = stage[b, 0], stage[b, 1]
                images += [re_a * re_b + im_a * im_b, im_a * re_b - re_a * im_b]
            at = pl.multiple_of(power_rows + r * (4 * ROWS), 2 * ROWS)
            keep_split(fields, pl.ds(at, 4 * ROWS), jnp.concatenate(images, axis=0), par)
            for f in range(4):
                keep(image, 4 * r + f, images[f])
            return carry

        lax.fori_loop(0, starts, product, 0, unroll=True)

        def looks():
            add_looks(acc_ifg, image, look_i[j], 4 * starts)

        if not tile:
            looks()
            return
        pl.when(j < BLOCKS)(looks)
        total = dot(fields[...], band[par + 2 * wrap])
        for f in range(held + 4 * starts):
            for h in range(2):
                sums[f, h, 8:48] = total[f * ROWS : (f + 1) * ROWS, h * 128 : (h + 1) * 128]

        def root(i, carry):
            for e in range(2):
                inv[2 * i + e] = lax.rsqrt(row_window(2 * i + e))
            return carry

        lax.fori_loop(0, held // 2, root, 0, unroll=True)

        def divide(r, carry):
            part = [row_window(held + 4 * r + f) for f in range(4)]
            inv_a = inv[jnp.where(r < GAP, r, r + GAP)]
            for q in range(2):
                square = part[2 * q] * part[2 * q] + part[2 * q + 1] * part[2 * q + 1]
                size = square * lax.rsqrt(jnp.maximum(square, 1e-37))
                keep(ratio, 2 * r + q, size * inv_a * inv[plan[0, 2 * r + q]])
            return carry

        lax.fori_loop(0, starts, divide, 0, unroll=True)
        add_looks(acc_coh, ratio, look_c[j], ratio.shape[0])

    step(0, False)

    def later(j, carry):
        step(j, True)
        return carry

    lax.fori_loop(1, BLOCKS + 1, later, 0)

    for r in range(starts):
        for q in range(2):
            target = res if r < GAP else res_far
            slot = 2 * r + q if r < GAP else 2 * (r - GAP) + q
            for f in range(3):
                if f < 2:
                    total = acc_ifg[8 * (4 * r + 2 * q + f) : 8 * (4 * r + 2 * q + f) + 8]
                else:
                    total = acc_coh[8 * (2 * r + q) : 8 * (2 * r + q) + 8]
                target[slot, f] = total / 100.0

    @pl.when(has_nb)
    def _():
        results().start()
        results().wait_recv()

    for p in range(2 * GAP):
        here = plan[1, p] == 1
        back = res_in[plan[2, p]]
        value = jnp.where(here, res[p], back)
        out_ifg[p] = value[0:2]
        out_coh[p] = value[2]

    def sent_all(j, carry):
        to_sib(j).wait_send()

        @pl.when(has_nb & (j >= BLOCKS - WINDOW))
        def _():
            to_nb(j).wait_send()

        @pl.when(is_relay & by_relay(j))
        def _():
            relay(j).wait_send()

        return carry

    lax.fori_loop(0, BLOCKS, sent_all, 0)
    halo_to(0).wait_send()

    @pl.when(has_nb)
    def _():
        halo_to(1).wait_send()
        results().wait_send()

    @pl.when(has_left)
    def _():
        to_side(0).wait_send()

    @pl.when(has_right)
    def _():
        to_side(1).wait_send()


def main_call(cross, table, slc):
    starts = GAP + cross
    held = 2 * GAP + cross + cross % 2
    rows = held * ROWS + starts * 4 * ROWS
    ratios = (2 * starts + 3) // 4 * 4
    vmem, dma = pltpu.VMEM, pltpu.SemaphoreType.DMA
    return pl.pallas_call(
        functools.partial(main_kernel, cross),
        out_shape=(
            jax.ShapeDtypeStruct((2 * GAP, 2, 8, 128), F32),
            jax.ShapeDtypeStruct((2 * GAP, 8, 128), F32),
        ),
        in_specs=[pl.BlockSpec(memory_space=pltpu.SMEM), pl.BlockSpec(memory_space=pl.ANY)],
        out_specs=(pl.BlockSpec(memory_space=vmem), pl.BlockSpec(memory_space=vmem)),
        scratch_shapes=[
            vmem((GAP, 2, ROWS, WIDTH), F32),
            vmem((GAP + cross, 2, ROWS, WIDTH), F32),
            vmem((cross, 2, ROWS, WIDTH), F32),
            vmem((held, 2, ROWS, BLOCK), F32),
            vmem((rows, 4 * BLOCK), BF16),
            vmem((held + 4 * starts, 2, 56, 128), F32),
            vmem((4 * starts, 2, ROWS, 128), F32),
            vmem((ratios, 2, ROWS, 128), F32),
            vmem((8 * 4 * starts, 2 * BLOCK), BF16),
            vmem((held, ROWS, BLOCK), F32),
            vmem((8 * 4 * starts, 128), F32),
            vmem((8 * ratios, 128), F32),
            vmem((BLOCKS + 1, 2 * BLOCK, 128), BF16),
            vmem((BLOCKS + 1, 2 * BLOCK, 128), BF16),
            vmem((3, 4 * BLOCK, BLOCK), BF16),
            vmem((cross, 2, ROWS, WIDTH), F32),
            vmem((4, ROWS, 128), F32),
            vmem((ROWS, 128), F32),
            vmem((2, ROWS, 128), F32),
            vmem((held, 2, ROWS, 128), F32),
            vmem((GAP, 2, ROWS, 128), F32),
            vmem((2 * GAP, 3, 8, 128), F32),
            vmem((2 * cross, 3, 8, 128), F32),
            vmem((2 * cross, 3, 8, 128), F32),
            pltpu.SMEM((3, 2 * starts), jnp.int32),
            dma,
            dma((BLOCKS,)),
            dma((BLOCKS,)),
            dma((BLOCKS,)),
            dma((BLOCKS,)),
            dma((2,)),
            dma((2,)),
            dma((2,)),
            dma((2,)),
            dma,
            dma,
            dma((BLOCKS,)),
            dma((BLOCKS,)),
        ],
        compiler_params=pltpu.CompilerParams(
            collective_id=cross, has_side_effects=True, vmem_limit_bytes=48 * 2**20
        ),
        name="pairs_" + str(cross),
    )(table, slc)


def body(slc, pairs):
    table = pl.pallas_call(
        plan_kernel,
        out_shape=jax.ShapeDtypeStruct((8, 128), jnp.int32),
        in_specs=[pl.BlockSpec(memory_space=pltpu.VMEM)],
        out_specs=pl.BlockSpec(memory_space=pltpu.VMEM),
        name="plan",
    )(pairs.T)
    return lax.cond(
        table[0, 127] == 0,
        functools.partial(main_call, 2),
        functools.partial(main_call, 3),
        table,
        slc,
    )


def solution(mesh):
    in_specs = (P("date", None, None, "col"), P())
    out_specs = (P("date", None, None, "col"), P("date", None, "col"))
    return jax.shard_map(body, mesh=mesh, in_specs=in_specs, out_specs=out_specs, check_vma=False)
```

```python
import functools

import jax
import jax.numpy as jnp
from jax import lax
from jax.experimental import pallas as pl
from jax.experimental.pallas import tpu as pltpu
from jax.sharding import PartitionSpec as P

GAP = 5
HALF = 5
ROWS = 40
WIDTH = 2560
BLOCK = 256
BLOCKS = WIDTH // BLOCK
LOOK_C = 20
WINDOW = 3
MESH = pl.DeviceIdType.MESH
F32 = jnp.float32
BF16 = jnp.bfloat16


def plan_kernel(pairs_ref, tab_ref):
    rows = pairs_ref.shape[1]
    lane = lax.broadcasted_iota(jnp.int32, (rows, 128), 1)
    row = lax.broadcasted_iota(jnp.int32, (rows, 128), 0)
    second = jnp.broadcast_to(pairs_ref[1:2, :], (8, rows)).astype(F32).astype(BF16)
    lane8 = lax.broadcasted_iota(jnp.int32, (8, 128), 1)
    row8 = lax.broadcasted_iota(jnp.int32, (8, 128), 0)
    sec, dist = [], []
    for q in range(2):
        pick = jnp.where(row == 2 * lane + q, 1.0, 0.0).astype(BF16)
        s = dot(second, pick).astype(jnp.int32)
        sec.append(s)
        dist.append(jnp.where(lane8 < rows // 2, s - lane8, 0))
    up = jnp.zeros((8, 128), jnp.int32)
    for k in range(1, GAP + 1):
        fwd = jnp.where((dist[0] == k) | (dist[1] == k), 1, 0)
        back = jnp.where((dist[0] == -k) | (dist[1] == -k), 1, 0)
        up = up | ((fwd | pltpu.roll(back, 128 - k, 1)) << (k - 1))
    masks = [pltpu.roll(up, GAP - i, 1) >> (GAP - 1 - i) for i in range(GAP)]
    found = jnp.zeros((8, 128), jnp.int32)
    s0 = jnp.zeros((8, 128), jnp.int32)
    s1 = jnp.ones((8, 128), jnp.int32)
    need = jnp.zeros((8, 128), jnp.int32)
    for lo in range(GAP - 2, -1, -1):
        for hi in range(GAP - 1, lo, -1):
            rest = jnp.zeros((8, 128), jnp.int32)
            for i in range(GAP):
                if i not in (lo, hi):
                    rest = rest | masks[i]
            count = jnp.zeros((8, 128), jnp.int32)
            for j in range(GAP):
                count = count + ((rest >> j) & 1)
            take = (count <= 2) & (found == 0)
            s0 = jnp.where(take, lo, s0)
            s1 = jnp.where(take, hi, s1)
            need = jnp.where(take, rest, need)
            found = jnp.where(take, 1, found)
    t0 = jnp.zeros((8, 128), jnp.int32)
    t1 = jnp.zeros((8, 128), jnp.int32)
    for j in range(GAP):
        t1 = jnp.where(((need >> j) & 1) == 1, j, t1)
        t0 = jnp.where(((need >> (GAP - 1 - j)) & 1) == 1, GAP - 1 - j, t0)
    chip = (lane8 % (2 * GAP) == 0) & (lane8 > 0) & (lane8 < rows // 2)
    missing = jnp.where(chip & (found == 0), 1.0, 0.0)
    wide = jnp.broadcast_to(jnp.max(missing, axis=1, keepdims=True), (8, 128)) > 0.5
    picks = [
        jnp.where(wide, 2, s0),
        jnp.where(wide, 3, s1),
        jnp.where(wide, 4, 0),
        jnp.where(wide, 0, t0),
        jnp.where(wide, 1, t1),
        jnp.zeros((8, 128), jnp.int32),
        sec[0],
        sec[1],
    ]
    table = jnp.zeros((8, 128), jnp.int32)
    for r, value in enumerate(picks):
        table = jnp.where(row8 == r, value, table)
    tab_ref[...] = jnp.where((lane8 == 127) & (row8 == 0), jnp.where(wide, 1, 0), table)


def split(x):
    hi = x.astype(BF16)
    return hi, (x - hi.astype(F32)).astype(BF16)


def dot(a, b):
    return jnp.dot(a, b, preferred_element_type=F32)


def main_kernel(
    cross, tab, slc, out_ifg, out_coh,
    own, dates, sent, stage, fields, sums, image, ratio, look_rows, inv, acc_ifg, acc_coh, look_i, look_c, band,
    relayed, edge, halo, other, tiles, tiles_nb, res, res_far, res_in, plan,
    load_sem, sib_send, sib_recv, nb_send, nb_recv, edge_send, edge_recv, halo_send, halo_recv, res_send, res_recv,
    relay_send, relay_recv,
):
    held = stage.shape[0]
    starts = GAP + cross
    power_rows = held * ROWS
    d, c = lax.axis_index("date"), lax.axis_index("col")
    n_d, n_c = lax.axis_size("date"), lax.axis_size("col")
    odd = lax.rem(d, 2)
    sib = d + 1 - 2 * odd
    nb = d - 1 + 2 * odd
    has_nb = (nb >= 0) & (nb < n_d)
    has_left, has_right = c > 0, c < n_c - 1

    kind = lax.rem(d, 4)
    onward = kind % 2 == 1
    relay_by = jnp.where(onward, d + 3, d - 3)
    relay_to = jnp.where(kind < 2, d + 2, d - 2)
    shared = (relay_by >= 0) & (relay_by < n_d)
    is_relay = shared & ((kind == 1) | (kind == 2))
    is_end = shared & ((kind == 0) | (kind == 3))
    line = lax.div(d, 4) - jnp.where(onward, 0, 1)
    share = jnp.where(kind >= 2, line, 2 - line)

    def by_relay(j):
        few = (j == 1) | (j == 4) | (j == 7)
        half = (j == 0) | (j == 2) | (j == 4) | (j == 6) | (j == 8)
        most = (j == 0) | (j == 1) | (j == 2) | (j == 4) | (j == 5) | (j == 7) | (j == 8)
        return ((share == 0) & few) | ((share == 1) & half) | ((share == 2) & most)

    load = pltpu.make_async_copy(slc, own, load_sem)
    load.start()

    barrier = pltpu.get_barrier_semaphore()
    pl.semaphore_signal(barrier, inc=1, device_id=(sib, c), device_id_type=MESH)

    @pl.when(has_nb)
    def _():
        pl.semaphore_signal(barrier, inc=1, device_id=(nb, c), device_id_type=MESH)

    @pl.when(shared)
    def _():
        pl.semaphore_signal(barrier, inc=1, device_id=(relay_by, c), device_id_type=MESH)
        pl.semaphore_signal(barrier, inc=1, device_id=(relay_to, c), device_id_type=MESH)

    @pl.when(has_left)
    def _():
        pl.semaphore_signal(barrier, inc=1, device_id=(d, c - 1), device_id_type=MESH)

    @pl.when(has_right)
    def _():
        pl.semaphore_signal(barrier, inc=1, device_id=(d, c + 1), device_id_type=MESH)

    lane_of = 5 * (d + odd)
    sel_out = [tab[3 * (1 - odd) + s, lane_of] for s in range(cross)]
    sel_in = [tab[3 * odd + s, lane_of] for s in range(cross)]
    greeted = 1 + jnp.where(has_nb, 1, 0) + jnp.where(has_left, 1, 0) + jnp.where(has_right, 1, 0)
    pl.semaphore_wait(barrier, greeted + jnp.where(shared, 2, 0))
    load.wait()

    def at_block(j):
        return pl.ds(pl.multiple_of(j * BLOCK, BLOCK), BLOCK)

    def to_sib(j):
        return pltpu.make_async_remote_copy(
            own.at[:, :, :, at_block(j)], dates.at[0:GAP, :, :, at_block(j)],
            sib_send.at[j], sib_recv.at[j], device_id=(sib, c), device_id_type=MESH,
        )

    def to_nb(j):
        return pltpu.make_async_remote_copy(
            sent.at[:, :, :, at_block(j)], dates.at[GAP : GAP + cross, :, :, at_block(j)],
            nb_send.at[j], nb_recv.at[j], device_id=(nb, c), device_id_type=MESH,
        )

    def to_relay(j):
        return pltpu.make_async_remote_copy(
            sent.at[:, :, :, at_block(j)], relayed.at[:, :, :, at_block(j)],
            nb_send.at[j], relay_recv.at[j], device_id=(relay_by, c), device_id_type=MESH,
        )

    def relay(j):
        return pltpu.make_async_remote_copy(
            relayed.at[:, :, :, at_block(j)], dates.at[GAP : GAP + cross, :, :, at_block(j)],
            relay_send.at[j], nb_recv.at[j], device_id=(relay_to, c), device_id_type=MESH,
        )

    def start_out(j):
        around = is_end & by_relay(j)

        @pl.when(has_nb & jnp.logical_not(around))
        def _():
            to_nb(j).start()

        @pl.when(around)
        def _():
            to_relay(j).start()

    def pass_on(j):
        @pl.when(is_relay & by_relay(j))
        def _():
            to_relay(j).wait_recv()
            relay(j).start()

    def to_side(side):
        return pltpu.make_async_remote_copy(
            edge.at[side], edge.at[2 + side], edge_send.at[side], edge_recv.at[side],
            device_id=(d, c - 1 if side == 0 else c + 1), device_id_type=MESH,
        )

    def halo_to(which):
        return pltpu.make_async_remote_copy(
            halo, other.at[which], halo_send.at[which], halo_recv.at[which],
            device_id=(sib if which == 0 else nb, c), device_id_type=MESH,
        )

    def results():
        return pltpu.make_async_remote_copy(
            res_far, res_in, res_send, res_recv, device_id=(nb, c), device_id_type=MESH
        )

    def send(j, carry):
        for s in range(cross):
            sent[s, :, :, at_block(j)] = own[sel_out[s], :, :, at_block(j)]

        pl.when(j < WINDOW)(lambda: start_out(j))
        to_sib(j).start()
        return carry

    lax.fori_loop(0, BLOCKS, send, 0)

    for r in range(GAP):
        for q in range(2):
            b = tab[6 + q, GAP * d + r]
            mine, sibling, far = b - GAP * d, b - GAP * sib, b - GAP * nb
            in_own = (mine >= 0) & (mine < GAP)
            in_sib = (sibling >= 0) & (sibling < GAP)
            place, here, back = jnp.int32(0), jnp.int32(0), jnp.int32(0)
            for s in range(cross):
                match = has_nb & (sel_in[s] == far)
                place = jnp.where(match, 2 * GAP + s, place)
                here = jnp.where(match, 1, here)
                back = jnp.where(sel_out[s] == r, 2 * s + q, back)
            place = jnp.where(in_own, mine, jnp.where(in_sib, GAP + sibling, place))
            here = jnp.where(in_own | in_sib, 1, here)
            plan[0, 2 * r + q] = place
            plan[1, 2 * r + q] = here
            plan[2, 2 * r + q] = back
    for s in range(cross):
        for q in range(2):
            far_date = jnp.clip(GAP * nb + sel_in[s], 0, GAP * n_d - 1)
            mine = tab[6 + q, far_date] - GAP * d
            plan[0, 2 * (GAP + s) + q] = jnp.where((mine >= 0) & (mine < GAP), mine, 0)

    k = lax.broadcasted_iota(jnp.int32, (BLOCK, BLOCK), 0)
    n = lax.broadcasted_iota(jnp.int32, (BLOCK, BLOCK), 1)
    near = lambda x: jnp.abs(x) <= HALF
    left_half = n < BLOCK // 2
    wrapped = jnp.where(
        left_half,
        jnp.where((k >= 246) & (k < 251) & near(k - 246 - (n - 128)), 1.0, 0.0),
        jnp.where(((k < 246) & near(k - n + 128)) | ((k >= 251) & near(k - 256 - n + 128)), 1.0, 0.0),
    )
    matrices = [
        jnp.where(near(k - n + 128), 1.0, 0.0),
        jnp.where(near(k - n - 128), 1.0, 0.0),
        wrapped,
        jnp.where(left_half & near(k - n - 128), 1.0, 0.0),
    ]
    for variant, order in enumerate(((0, 1), (1, 0), (2, 3))):
        for e in range(4):
            band[variant, e * BLOCK : (e + 1) * BLOCK] = matrices[order[e // 2]].astype(BF16)

    def fill_look(j, carry):
        column = lax.broadcasted_iota(jnp.int32, (BLOCK, 128), 0) + j * BLOCK
        first = lax.broadcasted_iota(jnp.int32, (BLOCK, 128), 1) * LOOK_C
        at = column - first
        ifg = jnp.where((at >= 0) & (at < LOOK_C), 1.0, 0.0).astype(BF16)
        at = column - BLOCK // 2
        at = jnp.where(at >= WIDTH, at - WIDTH, at) - first
        shifted = jnp.where((at >= 0) & (at < LOOK_C), 1.0, 0.0).astype(BF16)
        for e in range(2):
            look_i[j, e * BLOCK : (e + 1) * BLOCK] = ifg
            look_c[j, e * BLOCK : (e + 1) * BLOCK] = shifted
        return carry

    lax.fori_loop(0, BLOCKS + 1, fill_look, 0)
    acc_ifg[...] = jnp.zeros_like(acc_ifg)
    acc_coh[...] = jnp.zeros_like(acc_coh)
    ratio[...] = jnp.zeros_like(ratio)
    sums[:, :, 0:8] = jnp.zeros((sums.shape[0], 2, 8, 128), F32)
    sums[:, :, 48:56] = jnp.zeros((sums.shape[0], 2, 8, 128), F32)

    @pl.when(jnp.logical_not(has_nb))
    def _():
        dates[GAP : GAP + cross] = jnp.zeros((cross, 2, ROWS, WIDTH), F32)
        other[1] = jnp.zeros((ROWS, 128), F32)
        res_in[...] = jnp.zeros_like(res_in)

    if held > 2 * GAP + cross:
        stage[held - 1] = jnp.zeros((2, ROWS, BLOCK), F32)
        tiles[held - 1] = jnp.zeros((2, ROWS, 128), F32)


    lane = lax.broadcasted_iota(jnp.int32, (ROWS, 128), 1)
    left_edge = jnp.zeros((ROWS, 128), F32)
    right_edge = jnp.zeros((ROWS, 128), F32)
    for m in range(2 * GAP):
        tile = pltpu.roll(own[m // 2, m % 2, :, 0:128], 64 + 5 * m, 1)
        left_edge = jnp.where((lane >= 64 + 5 * m) & (lane < 69 + 5 * m), tile, left_edge)
        tile = pltpu.roll(own[m // 2, m % 2, :, WIDTH - 128 : WIDTH], 5 * m + 5, 1)
        right_edge = jnp.where((lane >= 5 * m) & (lane < 5 * m + 5), tile, right_edge)
    edge[0] = left_edge
    edge[1] = right_edge

    @pl.when(has_left)
    def _():
        to_side(0).start()

    @pl.when(has_right)
    def _():
        to_side(1).start()

    def forward_halo():
        @pl.when(has_right)
        def _():
            to_side(0).wait_recv()

        @pl.when(has_left)
        def _():
            to_side(1).wait_recv()

        @pl.when(jnp.logical_not(has_right))
        def _():
            edge[2] = jnp.zeros((ROWS, 128), F32)

        @pl.when(jnp.logical_not(has_left))
        def _():
            edge[3] = jnp.zeros((ROWS, 128), F32)

        halo[...] = jnp.where(lane < 64, edge[3], edge[2])
        halo_to(0).start()

        @pl.when(has_nb)
        def _():
            halo_to(1).start()

    def unpack_halo():
        halo_to(0).wait_recv()

        @pl.when(has_nb)
        def _():
            halo_to(1).wait_recv()

        for source in range(3):
            packed = halo[...] if source == 0 else other[source - 1]
            for m in range(2 * GAP):
                right = pltpu.roll(packed, (54 - 5 * m) % 128, 1)
                left = pltpu.roll(packed, (123 - 5 * m) % 128, 1)
                tile = jnp.where(lane < 123, right, left)
                if source < 2:
                    tiles[GAP * source + m // 2, m % 2] = tile
                else:
                    tiles_nb[m // 2, m % 2] = tile
        for s in range(cross):
            tiles[2 * GAP + s] = tiles_nb[sel_in[s]]

    def keep_split(target, rows, x, par=0):
        hi, lo = split(x)
        target[rows, pl.ds(pl.multiple_of(par * 2 * BLOCK, BLOCK), BLOCK)] = hi
        target[rows, pl.ds(pl.multiple_of(par * 2 * BLOCK + BLOCK, BLOCK), BLOCK)] = lo

    def row_window(f):
        halves = []
        for h in range(2):
            total = None
            for o in range(3, 11):
                if o < 6:
                    x = sums[f, h, o : o + 48]
                    x = x[0:ROWS] + x[8:48]
                else:
                    x = sums[f, h, o : o + ROWS]
                total = x if total is None else total + x
            halves.append(total)
        return jnp.concatenate(halves, axis=1)

    def keep(target, f, x):
        for h in range(2):
            target[f, h] = x[:, h * 128 : (h + 1) * 128]

    def add_looks(acc, source, look, count, first=0):
        def rows(i, carry):
            fields_of = []
            for e in range(4):
                halves = []
                for h in range(2):
                    total = source[first + 4 * i + e, h, pl.ds(0, 8, stride=5), :]
                    for o in range(1, 5):
                        total = total + source[first + 4 * i + e, h, pl.ds(o, 8, stride=5), :]
                    halves.append(total)
                fields_of.append(jnp.concatenate(halves, axis=1))
            at = pl.multiple_of(i * 32, 32)
            keep_split(look_rows, pl.ds(at, 32), jnp.concatenate(fields_of, axis=0))
            return carry

        lax.fori_loop(0, count // 4, rows, 0, unroll=True)
        acc[8 * first : 8 * (first + count)] += dot(look_rows[0 : 8 * count], look)

    far_slots = (2 * cross + 3) // 4 * 4

    def ratio_slot(r, q):
        return far_slots + 2 * r + q if r < GAP else 2 * (r - GAP) + q

    def means(dates_of):
        for r in dates_of:
            for q in range(2):
                target = res if r < GAP else res_far
                slot = 2 * r + q if r < GAP else 2 * (r - GAP) + q
                for f in range(3):
                    if f < 2:
                        at = 8 * (4 * r + 2 * q + f)
                        total = acc_ifg[at : at + 8]
                    else:
                        at = 8 * ratio_slot(r, q)
                        total = acc_coh[at : at + 8]
                    target[slot, f] = total / 100.0

    def step(j, tile):
        par = lax.rem(j, 2) if tile else 0
        wrap = jnp.where(j == BLOCKS, 1, 0) if tile else 0
        block = jnp.where(j == BLOCKS, 0, j) if tile else 0

        def arrive():
            to_sib(j).wait_recv()

            @pl.when(has_nb)
            def _():
                to_nb(j).wait_recv()

        if tile:
            pl.when(j + 2 < BLOCKS)(lambda: pass_on(j + 2))
            pl.when(j < BLOCKS)(arrive)
            pl.when(j == 2)(forward_halo)
            pl.when(j == 6)(unpack_halo)
        else:
            pass_on(0)
            pass_on(1)
            pass_on(2)
            arrive()

        for date in range(2 * GAP + cross):
            source = own.at[date] if date < GAP else dates.at[date - GAP]
            stage[date] = source[:, :, at_block(block)]
        if tile:

            @pl.when(j == BLOCKS)
            def _():
                for date in range(held):
                    for part in range(2):
                        stage[date, part, :, 128:256] = jnp.where(
                            lane < 118, stage[date, part, :, 128:256], tiles[date, part]
                        )

        @pl.when(j + WINDOW < BLOCKS)
        def _():
            @pl.when(has_nb)
            def _():
                to_nb(j).wait_send()

            start_out(j + WINDOW)

        def power(i, carry):
            both = []
            for e in range(2):
                re, im = stage[2 * i + e, 0], stage[2 * i + e, 1]
                both.append(re * re + im * im)
            at = pl.multiple_of(i * (2 * ROWS), 2 * ROWS)
            keep_split(fields, pl.ds(at, 2 * ROWS), jnp.concatenate(both, axis=0), par)
            return carry

        lax.fori_loop(0, held // 2, power, 0)

        def product(r, carry):
            a = jnp.where(r < GAP, r, r + GAP)
            re_a, im_a = stage[a, 0], stage[a, 1]
            images = []
            for q in range(2):
                b = plan[0, 2 * r + q]
                re_b, im_b = stage[b, 0], stage[b, 1]
                images += [re_a * re_b + im_a * im_b, im_a * re_b - re_a * im_b]
            at = pl.multiple_of(power_rows + r * (4 * ROWS), 2 * ROWS)
            keep_split(fields, pl.ds(at, 4 * ROWS), jnp.concatenate(images, axis=0), par)
            for f in range(4):
                keep(image, 4 * r + f, images[f])
            return carry

        lax.fori_loop(0, starts, product, 0, unroll=True)

        def looks():
            add_looks(acc_ifg, image, look_i[j], 4 * starts)

        if not tile:
            looks()
            return
        pl.when(j < BLOCKS)(looks)
        total = dot(fields[...], band[par + 2 * wrap])
        for f in range(held + 4 * starts):
            for h in range(2):
                sums[f, h, 8:48] = total[f * ROWS : (f + 1) * ROWS, h * 128 : (h + 1) * 128]

        def root(i, carry):
            for e in range(2):
                inv[2 * i + e] = lax.rsqrt(row_window(2 * i + e))
            return carry

        lax.fori_loop(0, held // 2, root, 0, unroll=True)

        def divide(r, carry):
            part = [row_window(held + 4 * r + f) for f in range(4)]
            inv_a = inv[r if r < GAP else r + GAP]
            for q in range(2):
                square = part[2 * q] * part[2 * q] + part[2 * q + 1] * part[2 * q + 1]
                size = square * lax.rsqrt(jnp.maximum(square, 1e-37))
                keep(ratio, ratio_slot(r, q), size * inv_a * inv[plan[0, 2 * r + q]])
            return carry

        for r in range(GAP, starts):
            divide(r, 0)
        add_looks(acc_coh, ratio, look_c[j], far_slots)

        @pl.when(j == BLOCKS)
        def _():
            means(range(GAP, starts))

            @pl.when(has_nb)
            def _():
                results().start()

        for r in range(GAP):
            divide(r, 0)
        add_looks(acc_coh, ratio, look_c[j], ratio.shape[0] - far_slots, far_slots)

    step(0, False)

    def later(j, carry):
        step(j, True)
        return carry

    lax.fori_loop(1, BLOCKS + 1, later, 0)

    means(range(GAP))

    @pl.when(has_nb)
    def _():
        results().wait_recv()

    for p in range(2 * GAP):
        here = plan[1, p] == 1
        back = res_in[plan[2, p]]
        value = jnp.where(here, res[p], back)
        out_ifg[p] = value[0:2]
        out_coh[p] = value[2]

    def sent_all(j, carry):
        to_sib(j).wait_send()

        @pl.when(has_nb & (j >= BLOCKS - WINDOW))
        def _():
            to_nb(j).wait_send()

        @pl.when(is_relay & by_relay(j))
        def _():
            relay(j).wait_send()

        return carry

    lax.fori_loop(0, BLOCKS, sent_all, 0)
    halo_to(0).wait_send()

    @pl.when(has_nb)
    def _():
        halo_to(1).wait_send()
        results().wait_send()

    @pl.when(has_left)
    def _():
        to_side(0).wait_send()

    @pl.when(has_right)
    def _():
        to_side(1).wait_send()


def main_call(cross, table, slc):
    starts = GAP + cross
    held = 2 * GAP + cross + cross % 2
    rows = held * ROWS + starts * 4 * ROWS
    ratios = (2 * cross + 3) // 4 * 4 + (2 * GAP + 3) // 4 * 4
    vmem, dma = pltpu.VMEM, pltpu.SemaphoreType.DMA
    return pl.pallas_call(
        functools.partial(main_kernel, cross),
        out_shape=(
            jax.ShapeDtypeStruct((2 * GAP, 2, 8, 128), F32),
            jax.ShapeDtypeStruct((2 * GAP, 8, 128), F32),
        ),
        in_specs=[pl.BlockSpec(memory_space=pltpu.SMEM), pl.BlockSpec(memory_space=pl.ANY)],
        out_specs=(pl.BlockSpec(memory_space=vmem), pl.BlockSpec(memory_space=vmem)),
        scratch_shapes=[
            vmem((GAP, 2, ROWS, WIDTH), F32),
            vmem((GAP + cross, 2, ROWS, WIDTH), F32),
            vmem((cross, 2, ROWS, WIDTH), F32),
            vmem((held, 2, ROWS, BLOCK), F32),
            vmem((rows, 4 * BLOCK), BF16),
            vmem((held + 4 * starts, 2, 56, 128), F32),
            vmem((4 * starts, 2, ROWS, 128), F32),
            vmem((ratios, 2, ROWS, 128), F32),
            vmem((8 * 4 * starts, 2 * BLOCK), BF16),
            vmem((held, ROWS, BLOCK), F32),
            vmem((8 * 4 * starts, 128), F32),
            vmem((8 * ratios, 128), F32),
            vmem((BLOCKS + 1, 2 * BLOCK, 128), BF16),
            vmem((BLOCKS + 1, 2 * BLOCK, 128), BF16),
            vmem((3, 4 * BLOCK, BLOCK), BF16),
            vmem((cross, 2, ROWS, WIDTH), F32),
            vmem((4, ROWS, 128), F32),
            vmem((ROWS, 128), F32),
            vmem((2, ROWS, 128), F32),
            vmem((held, 2, ROWS, 128), F32),
            vmem((GAP, 2, ROWS, 128), F32),
            vmem((2 * GAP, 3, 8, 128), F32),
            vmem((2 * cross, 3, 8, 128), F32),
            vmem((2 * cross, 3, 8, 128), F32),
            pltpu.SMEM((3, 2 * starts), jnp.int32),
            dma,
            dma((BLOCKS,)),
            dma((BLOCKS,)),
            dma((BLOCKS,)),
            dma((BLOCKS,)),
            dma((2,)),
            dma((2,)),
            dma((2,)),
            dma((2,)),
            dma,
            dma,
            dma((BLOCKS,)),
            dma((BLOCKS,)),
        ],
        compiler_params=pltpu.CompilerParams(
            collective_id=cross, has_side_effects=True, vmem_limit_bytes=48 * 2**20
        ),
        name="pairs_" + str(cross),
    )(table, slc)


def body(slc, pairs):
    table = pl.pallas_call(
        plan_kernel,
        out_shape=jax.ShapeDtypeStruct((8, 128), jnp.int32),
        in_specs=[pl.BlockSpec(memory_space=pltpu.VMEM)],
        out_specs=pl.BlockSpec(memory_space=pltpu.VMEM),
        name="plan",
    )(pairs.T)
    return lax.cond(
        table[0, 127] == 0,
        functools.partial(main_call, 2),
        functools.partial(main_call, 3),
        table,
        slc,
    )


def solution(mesh):
    in_specs = (P("date", None, None, "col"), P())
    out_specs = (P("date", None, None, "col"), P("date", None, "col"))
    return jax.shard_map(body, mesh=mesh, in_specs=in_specs, out_specs=out_specs, check_vma=False)
```

```python
import functools

import jax
import jax.numpy as jnp
from jax import lax
from jax.experimental import pallas as pl
from jax.experimental.pallas import tpu as pltpu
from jax.sharding import PartitionSpec as P

GAP = 5
HALF = 5
ROWS = 40
WIDTH = 2560
BLOCK = 256
BLOCKS = WIDTH // BLOCK
LOOK_C = 20
WINDOW = 3
MESH = pl.DeviceIdType.MESH
F32 = jnp.float32
BF16 = jnp.bfloat16


def plan_kernel(pairs_ref, tab_ref):
    rows = pairs_ref.shape[1]
    lane = lax.broadcasted_iota(jnp.int32, (rows, 128), 1)
    row = lax.broadcasted_iota(jnp.int32, (rows, 128), 0)
    second = jnp.broadcast_to(pairs_ref[1:2, :], (8, rows)).astype(F32).astype(BF16)
    lane8 = lax.broadcasted_iota(jnp.int32, (8, 128), 1)
    row8 = lax.broadcasted_iota(jnp.int32, (8, 128), 0)
    sec, dist = [], []
    for q in range(2):
        pick = jnp.where(row == 2 * lane + q, 1.0, 0.0).astype(BF16)
        s = dot(second, pick).astype(jnp.int32)
        sec.append(s)
        dist.append(jnp.where(lane8 < rows // 2, s - lane8, 0))
    up = jnp.zeros((8, 128), jnp.int32)
    for k in range(1, GAP + 1):
        fwd = jnp.where((dist[0] == k) | (dist[1] == k), 1, 0)
        back = jnp.where((dist[0] == -k) | (dist[1] == -k), 1, 0)
        up = up | ((fwd | pltpu.roll(back, 128 - k, 1)) << (k - 1))
    masks = [pltpu.roll(up, GAP - i, 1) >> (GAP - 1 - i) for i in range(GAP)]
    found = jnp.zeros((8, 128), jnp.int32)
    s0 = jnp.zeros((8, 128), jnp.int32)
    s1 = jnp.ones((8, 128), jnp.int32)
    need = jnp.zeros((8, 128), jnp.int32)
    for lo in range(GAP - 2, -1, -1):
        for hi in range(GAP - 1, lo, -1):
            rest = jnp.zeros((8, 128), jnp.int32)
            for i in range(GAP):
                if i not in (lo, hi):
                    rest = rest | masks[i]
            count = jnp.zeros((8, 128), jnp.int32)
            for j in range(GAP):
                count = count + ((rest >> j) & 1)
            take = (count <= 2) & (found == 0)
            s0 = jnp.where(take, lo, s0)
            s1 = jnp.where(take, hi, s1)
            need = jnp.where(take, rest, need)
            found = jnp.where(take, 1, found)
    t0 = jnp.zeros((8, 128), jnp.int32)
    t1 = jnp.zeros((8, 128), jnp.int32)
    for j in range(GAP):
        t1 = jnp.where(((need >> j) & 1) == 1, j, t1)
        t0 = jnp.where(((need >> (GAP - 1 - j)) & 1) == 1, GAP - 1 - j, t0)
    chip = (lane8 % (2 * GAP) == 0) & (lane8 > 0) & (lane8 < rows // 2)
    missing = jnp.where(chip & (found == 0), 1.0, 0.0)
    wide = jnp.broadcast_to(jnp.max(missing, axis=1, keepdims=True), (8, 128)) > 0.5
    picks = [
        jnp.where(wide, 2, s0),
        jnp.where(wide, 3, s1),
        jnp.where(wide, 4, 0),
        jnp.where(wide, 0, t0),
        jnp.where(wide, 1, t1),
        jnp.zeros((8, 128), jnp.int32),
        sec[0],
        sec[1],
    ]
    table = jnp.zeros((8, 128), jnp.int32)
    for r, value in enumerate(picks):
        table = jnp.where(row8 == r, value, table)
    tab_ref[...] = jnp.where((lane8 == 127) & (row8 == 0), jnp.where(wide, 1, 0), table)


def split(x):
    hi = x.astype(BF16)
    return hi, (x - hi.astype(F32)).astype(BF16)


def dot(a, b):
    return jnp.dot(a, b, preferred_element_type=F32)


def main_kernel(
    cross, tab, slc, out_ifg, out_coh,
    own, dates, sent, stage, fields, sums, image, ratio, look_rows, inv, acc_ifg, acc_coh, look_i, look_c, band,
    relayed, edge, halo, other, tiles, tiles_nb, res, res_far, res_in, plan,
    load_sem, sib_send, sib_recv, nb_send, nb_recv, edge_send, edge_recv, halo_send, halo_recv, res_send, res_recv,
    relay_send, relay_recv,
):
    held = stage.shape[0]
    starts = GAP + cross
    power_rows = held * ROWS
    d, c = lax.axis_index("date"), lax.axis_index("col")
    n_d, n_c = lax.axis_size("date"), lax.axis_size("col")
    odd = lax.rem(d, 2)
    sib = d + 1 - 2 * odd
    nb = d - 1 + 2 * odd
    has_nb = (nb >= 0) & (nb < n_d)
    has_left, has_right = c > 0, c < n_c - 1

    kind = lax.rem(d, 4)
    onward = kind % 2 == 1
    relay_by = jnp.where(onward, d + 3, d - 3)
    relay_to = jnp.where(kind < 2, d + 2, d - 2)
    shared = (relay_by >= 0) & (relay_by < n_d)
    is_relay = shared & ((kind == 1) | (kind == 2))
    is_end = shared & ((kind == 0) | (kind == 3))
    line = lax.div(d, 4) - jnp.where(onward, 0, 1)
    share = jnp.where(kind >= 2, line, 2 - line)

    def by_relay(j):
        few = (j == 1) | (j == 4) | (j == 7)
        half = (j == 0) | (j == 2) | (j == 4) | (j == 6) | (j == 8)
        most = (j == 0) | (j == 1) | (j == 2) | (j == 4) | (j == 5) | (j == 7) | (j == 8)
        return ((share == 0) & few) | ((share == 1) & half) | ((share == 2) & most)

    load = pltpu.make_async_copy(slc, own, load_sem)
    load.start()

    barrier = pltpu.get_barrier_semaphore()
    pl.semaphore_signal(barrier, inc=1, device_id=(sib, c), device_id_type=MESH)

    @pl.when(has_nb)
    def _():
        pl.semaphore_signal(barrier, inc=1, device_id=(nb, c), device_id_type=MESH)

    @pl.when(shared)
    def _():
        pl.semaphore_signal(barrier, inc=1, device_id=(relay_by, c), device_id_type=MESH)
        pl.semaphore_signal(barrier, inc=1, device_id=(relay_to, c), device_id_type=MESH)

    @pl.when(has_left)
    def _():
        pl.semaphore_signal(barrier, inc=1, device_id=(d, c - 1), device_id_type=MESH)

    @pl.when(has_right)
    def _():
        pl.semaphore_signal(barrier, inc=1, device_id=(d, c + 1), device_id_type=MESH)

    lane_of = 5 * (d + odd)
    sel_out = [tab[3 * (1 - odd) + s, lane_of] for s in range(cross)]
    sel_in = [tab[3 * odd + s, lane_of] for s in range(cross)]
    greeted = 1 + jnp.where(has_nb, 1, 0) + jnp.where(has_left, 1, 0) + jnp.where(has_right, 1, 0)
    pl.semaphore_wait(barrier, greeted + jnp.where(shared, 2, 0))
    load.wait()

    def at_block(j):
        return pl.ds(pl.multiple_of(j * BLOCK, BLOCK), BLOCK)

    def to_sib(j):
        return pltpu.make_async_remote_copy(
            own.at[:, :, :, at_block(j)], dates.at[0:GAP, :, :, at_block(j)],
            sib_send.at[j], sib_recv.at[j], device_id=(sib, c), device_id_type=MESH,
        )

    def to_nb(j):
        return pltpu.make_async_remote_copy(
            sent.at[:, :, :, at_block(j)], dates.at[GAP : GAP + cross, :, :, at_block(j)],
            nb_send.at[j], nb_recv.at[j], device_id=(nb, c), device_id_type=MESH,
        )

    def to_relay(j):
        return pltpu.make_async_remote_copy(
            sent.at[:, :, :, at_block(j)], relayed.at[:, :, :, at_block(j)],
            nb_send.at[j], relay_recv.at[j], device_id=(relay_by, c), device_id_type=MESH,
        )

    def relay(j):
        return pltpu.make_async_remote_copy(
            relayed.at[:, :, :, at_block(j)], dates.at[GAP : GAP + cross, :, :, at_block(j)],
            relay_send.at[j], nb_recv.at[j], device_id=(relay_to, c), device_id_type=MESH,
        )

    def start_out(j):
        around = is_end & by_relay(j)

        @pl.when(has_nb & jnp.logical_not(around))
        def _():
            to_nb(j).start()

        @pl.when(around)
        def _():
            to_relay(j).start()

    def pass_on(j):
        @pl.when(is_relay & by_relay(j))
        def _():
            to_relay(j).wait_recv()
            relay(j).start()

    def to_side(side):
        return pltpu.make_async_remote_copy(
            edge.at[side], edge.at[2 + side], edge_send.at[side], edge_recv.at[side],
            device_id=(d, c - 1 if side == 0 else c + 1), device_id_type=MESH,
        )

    def halo_to(which):
        return pltpu.make_async_remote_copy(
            halo, other.at[which], halo_send.at[which], halo_recv.at[which],
            device_id=(sib if which == 0 else nb, c), device_id_type=MESH,
        )

    def results():
        return pltpu.make_async_remote_copy(
            res_far, res_in, res_send, res_recv, device_id=(nb, c), device_id_type=MESH
        )

    def send(j, carry):
        for s in range(cross):
            sent[s, :, :, at_block(j)] = own[sel_out[s], :, :, at_block(j)]

        pl.when(j < WINDOW)(lambda: start_out(j))
        to_sib(j).start()
        return carry

    lax.fori_loop(0, BLOCKS, send, 0)

    for r in range(GAP):
        for q in range(2):
            b = tab[6 + q, GAP * d + r]
            mine, sibling, far = b - GAP * d, b - GAP * sib, b - GAP * nb
            in_own = (mine >= 0) & (mine < GAP)
            in_sib = (sibling >= 0) & (sibling < GAP)
            place, here, back = jnp.int32(0), jnp.int32(0), jnp.int32(0)
            for s in range(cross):
                match = has_nb & (sel_in[s] == far)
                place = jnp.where(match, 2 * GAP + s, place)
                here = jnp.where(match, 1, here)
                back = jnp.where(sel_out[s] == r, 2 * s + q, back)
            place = jnp.where(in_own, mine, jnp.where(in_sib, GAP + sibling, place))
            here = jnp.where(in_own | in_sib, 1, here)
            plan[0, 2 * r + q] = place
            plan[1, 2 * r + q] = here
            plan[2, 2 * r + q] = back
    for s in range(cross):
        for q in range(2):
            far_date = jnp.clip(GAP * nb + sel_in[s], 0, GAP * n_d - 1)
            mine = tab[6 + q, far_date] - GAP * d
            plan[0, 2 * (GAP + s) + q] = jnp.where((mine >= 0) & (mine < GAP), mine, 0)

    k = lax.broadcasted_iota(jnp.int32, (BLOCK, BLOCK), 0)
    n = lax.broadcasted_iota(jnp.int32, (BLOCK, BLOCK), 1)
    near = lambda x: jnp.abs(x) <= HALF
    left_half = n < BLOCK // 2
    wrapped = jnp.where(
        left_half,
        jnp.where((k >= 246) & (k < 251) & near(k - 246 - (n - 128)), 1.0, 0.0),
        jnp.where(((k < 246) & near(k - n + 128)) | ((k >= 251) & near(k - 256 - n + 128)), 1.0, 0.0),
    )
    matrices = [
        jnp.where(near(k - n + 128), 1.0, 0.0),
        jnp.where(near(k - n - 128), 1.0, 0.0),
        wrapped,
        jnp.where(left_half & near(k - n - 128), 1.0, 0.0),
    ]
    for variant, order in enumerate(((0, 1), (1, 0), (2, 3))):
        for e in range(4):
            band[variant, e * BLOCK : (e + 1) * BLOCK] = matrices[order[e // 2]].astype(BF16)

    def fill_look(j, carry):
        column = lax.broadcasted_iota(jnp.int32, (BLOCK, 128), 0) + j * BLOCK
        first = lax.broadcasted_iota(jnp.int32, (BLOCK, 128), 1) * LOOK_C
        at = column - first
        ifg = jnp.where((at >= 0) & (at < LOOK_C), 1.0, 0.0).astype(BF16)
        at = column - BLOCK // 2
        at = jnp.where(at >= WIDTH, at - WIDTH, at) - first
        shifted = jnp.where((at >= 0) & (at < LOOK_C), 1.0, 0.0).astype(BF16)
        for e in range(2):
            look_i[j, e * BLOCK : (e + 1) * BLOCK] = ifg
            look_c[j, e * BLOCK : (e + 1) * BLOCK] = shifted
        return carry

    lax.fori_loop(0, BLOCKS + 1, fill_look, 0)
    acc_ifg[...] = jnp.zeros_like(acc_ifg)
    acc_coh[...] = jnp.zeros_like(acc_coh)
    ratio[...] = jnp.zeros_like(ratio)
    sums[:, :, 0:8] = jnp.zeros((sums.shape[0], 2, 8, 128), F32)
    sums[:, :, 48:56] = jnp.zeros((sums.shape[0], 2, 8, 128), F32)

    @pl.when(jnp.logical_not(has_nb))
    def _():
        dates[GAP : GAP + cross] = jnp.zeros((cross, 2, ROWS, WIDTH), F32)
        other[1] = jnp.zeros((ROWS, 128), F32)
        res_in[...] = jnp.zeros_like(res_in)

    if held > 2 * GAP + cross:
        stage[held - 1] = jnp.zeros((2, ROWS, BLOCK), F32)
        tiles[held - 1] = jnp.zeros((2, ROWS, 128), F32)


    lane = lax.broadcasted_iota(jnp.int32, (ROWS, 128), 1)
    left_edge = jnp.zeros((ROWS, 128), F32)
    right_edge = jnp.zeros((ROWS, 128), F32)
    for m in range(2 * GAP):
        tile = pltpu.roll(own[m // 2, m % 2, :, 0:128], 64 + 5 * m, 1)
        left_edge = jnp.where((lane >= 64 + 5 * m) & (lane < 69 + 5 * m), tile, left_edge)
        tile = pltpu.roll(own[m // 2, m % 2, :, WIDTH - 128 : WIDTH], 5 * m + 5, 1)
        right_edge = jnp.where((lane >= 5 * m) & (lane < 5 * m + 5), tile, right_edge)
    edge[0] = left_edge
    edge[1] = right_edge

    @pl.when(has_left)
    def _():
        to_side(0).start()

    @pl.when(has_right)
    def _():
        to_side(1).start()

    def forward_halo():
        @pl.when(has_right)
        def _():
            to_side(0).wait_recv()

        @pl.when(has_left)
        def _():
            to_side(1).wait_recv()

        @pl.when(jnp.logical_not(has_right))
        def _():
            edge[2] = jnp.zeros((ROWS, 128), F32)

        @pl.when(jnp.logical_not(has_left))
        def _():
            edge[3] = jnp.zeros((ROWS, 128), F32)

        halo[...] = jnp.where(lane < 64, edge[3], edge[2])
        halo_to(0).start()

        @pl.when(has_nb)
        def _():
            halo_to(1).start()

    def unpack_halo():
        halo_to(0).wait_recv()

        @pl.when(has_nb)
        def _():
            halo_to(1).wait_recv()

        for source in range(3):
            packed = halo[...] if source == 0 else other[source - 1]
            for m in range(2 * GAP):
                right = pltpu.roll(packed, (54 - 5 * m) % 128, 1)
                left = pltpu.roll(packed, (123 - 5 * m) % 128, 1)
                tile = jnp.where(lane < 123, right, left)
                if source < 2:
                    tiles[GAP * source + m // 2, m % 2] = tile
                else:
                    tiles_nb[m // 2, m % 2] = tile
        for s in range(cross):
            tiles[2 * GAP + s] = tiles_nb[sel_in[s]]

    def keep_split(target, rows, x, par=0):
        hi, lo = split(x)
        target[rows, pl.ds(pl.multiple_of(par * 2 * BLOCK, BLOCK), BLOCK)] = hi
        target[rows, pl.ds(pl.multiple_of(par * 2 * BLOCK + BLOCK, BLOCK), BLOCK)] = lo

    def row_window(f):
        halves = []
        for h in range(2):
            total = None
            for o in range(3, 11):
                if o < 6:
                    x = sums[f, h, o : o + 48]
                    x = x[0:ROWS] + x[8:48]
                else:
                    x = sums[f, h, o : o + ROWS]
                total = x if total is None else total + x
            halves.append(total)
        return jnp.concatenate(halves, axis=1)

    def keep(target, f, x):
        for h in range(2):
            target[f, h, 0:ROWS] = x[:, h * 128 : (h + 1) * 128]

    def add_looks(acc, source, look, count, first=0):
        def rows(i, carry):
            fields_of = []
            for e in range(4):
                halves = []
                for h in range(2):
                    total = source[first + 4 * i + e, h, pl.ds(0, 8, stride=5), :]
                    for o in range(1, 5):
                        total = total + source[first + 4 * i + e, h, pl.ds(o, 8, stride=5), :]
                    halves.append(total)
                fields_of.append(jnp.concatenate(halves, axis=1))
            at = pl.multiple_of(i * 32, 32)
            keep_split(look_rows, pl.ds(at, 32), jnp.concatenate(fields_of, axis=0))
            return carry

        lax.fori_loop(0, count // 4, rows, 0, unroll=True)
        acc[8 * first : 8 * (first + count)] += dot(look_rows[0 : 8 * count], look)

    far_slots = (2 * cross + 3) // 4 * 4

    def ratio_slot(r, q):
        return far_slots + 2 * r + q if r < GAP else 2 * (r - GAP) + q

    def means(dates_of):
        for r in dates_of:
            for q in range(2):
                target = res if r < GAP else res_far
                slot = 2 * r + q if r < GAP else 2 * (r - GAP) + q
                for f in range(3):
                    if f < 2:
                        at = 8 * (4 * r + 2 * q + f)
                        total = acc_ifg[at : at + 8]
                    else:
                        at = 8 * ratio_slot(r, q)
                        total = acc_coh[at : at + 8]
                    target[slot, f] = total / 100.0

    def step(j, tile):
        par = lax.rem(j, 2) if tile else 0
        wrap = jnp.where(j == BLOCKS, 1, 0) if tile else 0
        block = jnp.where(j == BLOCKS, 0, j) if tile else 0

        def arrive():
            to_sib(j).wait_recv()

            @pl.when(has_nb)
            def _():
                to_nb(j).wait_recv()

        if tile:
            pl.when(j + 2 < BLOCKS)(lambda: pass_on(j + 2))
            pl.when(j < BLOCKS)(arrive)
            pl.when(j == 2)(forward_halo)
            pl.when(j == 6)(unpack_halo)
        else:
            pass_on(0)
            pass_on(1)
            pass_on(2)
            arrive()

        for date in range(2 * GAP + cross):
            source = own.at[date] if date < GAP else dates.at[date - GAP]
            stage[date] = source[:, :, at_block(block)]
        if tile:

            @pl.when(j == BLOCKS)
            def _():
                for date in range(held):
                    for part in range(2):
                        stage[date, part, :, 128:256] = jnp.where(
                            lane < 118, stage[date, part, :, 128:256], tiles[date, part]
                        )

        @pl.when(j + WINDOW < BLOCKS)
        def _():
            @pl.when(has_nb)
            def _():
                to_nb(j).wait_send()

            start_out(j + WINDOW)

        def power(i, carry):
            both = []
            for e in range(2):
                re, im = stage[2 * i + e, 0], stage[2 * i + e, 1]
                both.append(re * re + im * im)
            at = pl.multiple_of(i * (2 * ROWS), 2 * ROWS)
            keep_split(fields, pl.ds(at, 2 * ROWS), jnp.concatenate(both, axis=0), par)
            return carry

        lax.fori_loop(0, held // 2, power, 0)

        def product(r, carry):
            a = jnp.where(r < GAP, r, r + GAP)
            re_a, im_a = stage[a, 0], stage[a, 1]
            images = []
            for q in range(2):
                b = plan[0, 2 * r + q]
                re_b, im_b = stage[b, 0], stage[b, 1]
                images += [re_a * re_b + im_a * im_b, im_a * re_b - re_a * im_b]
            at = pl.multiple_of(power_rows + r * (4 * ROWS), 2 * ROWS)
            keep_split(fields, pl.ds(at, 4 * ROWS), jnp.concatenate(images, axis=0), par)
            for f in range(4):
                keep(image, 4 * r + f, images[f])
            return carry

        lax.fori_loop(0, starts, product, 0, unroll=True)

        def looks():
            add_looks(acc_ifg, image, look_i[j], 4 * starts)

        if not tile:
            looks()
            return
        pl.when(j < BLOCKS)(looks)
        total = dot(fields[...], band[par + 2 * wrap])
        for f in range(held + 4 * starts):
            for h in range(2):
                sums[f, h, 8:48] = total[f * ROWS : (f + 1) * ROWS, h * 128 : (h + 1) * 128]

        def root(i, carry):
            for e in range(2):
                inv[2 * i + e] = lax.rsqrt(row_window(2 * i + e))
            return carry

        lax.fori_loop(0, held // 2, root, 0, unroll=True)

        def divide(r, carry):
            part = [row_window(held + 4 * r + f) for f in range(4)]
            inv_a = inv[r if r < GAP else r + GAP]
            for q in range(2):
                square = part[2 * q] * part[2 * q] + part[2 * q + 1] * part[2 * q + 1]
                size = square * lax.rsqrt(jnp.maximum(square, 1e-37))
                keep(ratio, ratio_slot(r, q), size * inv_a * inv[plan[0, 2 * r + q]])
            return carry

        for r in range(GAP, starts):
            divide(r, 0)
        add_looks(acc_coh, ratio, look_c[j], far_slots)

        @pl.when(j == BLOCKS)
        def _():
            means(range(GAP, starts))

            @pl.when(has_nb)
            def _():
                results().start()

        for r in range(GAP):
            divide(r, 0)
        add_looks(acc_coh, ratio, look_c[j], ratio.shape[0] - far_slots, far_slots)

    step(0, False)

    def later(j, carry):
        step(j, True)
        return carry

    lax.fori_loop(1, BLOCKS + 1, later, 0)

    means(range(GAP))

    @pl.when(has_nb)
    def _():
        results().wait_recv()

    for p in range(2 * GAP):
        here = plan[1, p] == 1
        back = res_in[plan[2, p]]
        value = jnp.where(here, res[p], back)
        out_ifg[p] = value[0:2]
        out_coh[p] = value[2]

    def sent_all(j, carry):
        to_sib(j).wait_send()

        @pl.when(has_nb & (j >= BLOCKS - WINDOW))
        def _():
            to_nb(j).wait_send()

        @pl.when(is_relay & by_relay(j))
        def _():
            relay(j).wait_send()

        return carry

    lax.fori_loop(0, BLOCKS, sent_all, 0)
    halo_to(0).wait_send()

    @pl.when(has_nb)
    def _():
        halo_to(1).wait_send()
        results().wait_send()

    @pl.when(has_left)
    def _():
        to_side(0).wait_send()

    @pl.when(has_right)
    def _():
        to_side(1).wait_send()


def main_call(cross, table, slc):
    starts = GAP + cross
    held = 2 * GAP + cross + cross % 2
    rows = held * ROWS + starts * 4 * ROWS
    ratios = (2 * cross + 3) // 4 * 4 + (2 * GAP + 3) // 4 * 4
    vmem, dma = pltpu.VMEM, pltpu.SemaphoreType.DMA
    return pl.pallas_call(
        functools.partial(main_kernel, cross),
        out_shape=(
            jax.ShapeDtypeStruct((2 * GAP, 2, 8, 128), F32),
            jax.ShapeDtypeStruct((2 * GAP, 8, 128), F32),
        ),
        in_specs=[pl.BlockSpec(memory_space=pltpu.SMEM), pl.BlockSpec(memory_space=pl.ANY)],
        out_specs=(pl.BlockSpec(memory_space=vmem), pl.BlockSpec(memory_space=vmem)),
        scratch_shapes=[
            vmem((GAP, 2, ROWS, WIDTH), F32),
            vmem((GAP + cross, 2, ROWS, WIDTH), F32),
            vmem((cross, 2, ROWS, WIDTH), F32),
            vmem((held, 2, ROWS, BLOCK), F32),
            vmem((rows, 4 * BLOCK), BF16),
            vmem((held + 4 * starts, 2, 56, 128), F32),
            vmem((4 * starts, 2, ROWS + 8, 128), F32),
            vmem((ratios, 2, ROWS + 8, 128), F32),
            vmem((8 * 4 * starts, 2 * BLOCK), BF16),
            vmem((held, ROWS, BLOCK), F32),
            vmem((8 * 4 * starts, 128), F32),
            vmem((8 * ratios, 128), F32),
            vmem((BLOCKS + 1, 2 * BLOCK, 128), BF16),
            vmem((BLOCKS + 1, 2 * BLOCK, 128), BF16),
            vmem((3, 4 * BLOCK, BLOCK), BF16),
            vmem((cross, 2, ROWS, WIDTH), F32),
            vmem((4, ROWS, 128), F32),
            vmem((ROWS, 128), F32),
            vmem((2, ROWS, 128), F32),
            vmem((held, 2, ROWS, 128), F32),
            vmem((GAP, 2, ROWS, 128), F32),
            vmem((2 * GAP, 3, 8, 128), F32),
            vmem((2 * cross, 3, 8, 128), F32),
            vmem((2 * cross, 3, 8, 128), F32),
            pltpu.SMEM((3, 2 * starts), jnp.int32),
            dma,
            dma((BLOCKS,)),
            dma((BLOCKS,)),
            dma((BLOCKS,)),
            dma((BLOCKS,)),
            dma((2,)),
            dma((2,)),
            dma((2,)),
            dma((2,)),
            dma,
            dma,
            dma((BLOCKS,)),
            dma((BLOCKS,)),
        ],
        compiler_params=pltpu.CompilerParams(
            collective_id=cross, has_side_effects=True, vmem_limit_bytes=48 * 2**20
        ),
        name="pairs_" + str(cross),
    )(table, slc)


def body(slc, pairs):
    table = pl.pallas_call(
        plan_kernel,
        out_shape=jax.ShapeDtypeStruct((8, 128), jnp.int32),
        in_specs=[pl.BlockSpec(memory_space=pltpu.VMEM)],
        out_specs=pl.BlockSpec(memory_space=pltpu.VMEM),
        name="plan",
    )(pairs.T)
    return lax.cond(
        table[0, 127] == 0,
        functools.partial(main_call, 2),
        functools.partial(main_call, 3),
        table,
        slc,
    )


def solution(mesh):
    in_specs = (P("date", None, None, "col"), P())
    out_specs = (P("date", None, None, "col"), P("date", None, "col"))
    return jax.shard_map(body, mesh=mesh, in_specs=in_specs, out_specs=out_specs, check_vma=False)
```
